512 devices in a mesh: seq: 128 (over y, z, core), head: 4 (over x).
Axes of the slice: x: 4, y: 4, z: 16, core: 2. Of those that a mesh axis runs over, the one named last changes fastest.
Arguments:
- queries: bfloat16 [16384, 4096], P('seq', 'head'), may hold values from -6 to 6
- key_states: bfloat16 [16384, 4096], P('seq', 'head'), may hold values from -6 to 6
- value_states: bfloat16 [16384, 4096], P('seq', 'head'), may hold values from -6 to 6
- cotangent: bfloat16 [16384, 4096], P(('seq', 'head')), may hold values from -6 to 6
Outputs:
- attended: bfloat16 [16384, 4096], P(('seq', 'head'))
- query_gradient: bfloat16 [16384, 4096], P('seq', 'head')
- key_gradient: bfloat16 [16384, 4096], P('seq', 'head')
- value_gradient: bfloat16 [16384, 4096], P('seq', 'head')
The draws below stay inside these ranges and needn't reach their ends.
All inputs are finite; a program needn't handle non-finite values.
Results may differ from the reference program's by a relative error of at most 0.011.
Values may be sent and summed in bfloat16 or wider, within the bound.
No kernel may reach another device: no remote copies, remote signals or barrier semaphores. Data moves between devices by JAX's collectives and lax.ppermute only.
A program may use at most 64 MiB of HBM per device.

```python
import math
import jax
import jax.numpy as jnp
from jax import lax

HEADS = 32
HEAD_DIM = 128
BLOCK = 128
LEVELS = 4
SEQ = 16384
N_SEQ = 128


def draw_queries(key, part):
    key = jax.random.fold_in(key, 1)
    shape = (BLOCK * N_SEQ, HEADS * HEAD_DIM)
    return jnp.clip(jax.random.normal(key, shape, jnp.float32), -6.0, 6.0).astype(jnp.bfloat16)


def draw_key_states(key, part):
    key = jax.random.fold_in(key, 2)
    shape = (BLOCK * N_SEQ, HEADS * HEAD_DIM)
    return jnp.clip(jax.random.normal(key, shape, jnp.float32), -6.0, 6.0).astype(jnp.bfloat16)


def block_scale(stream_key, dims, pieces, low, high):
    gain, own = 1.0, jax.random.fold_in(stream_key, 6)
    for dim, blocks in pieces:
        draws = jnp.exp(jax.random.uniform(jax.random.fold_in(own, dim), (blocks,), jnp.float32, low / len(pieces), high / len(pieces)))
        gain = gain * jnp.repeat(draws, dims[dim] // blocks).reshape([-1 if axis == dim else 1 for axis in range(len(dims))])
    return gain


def scatter_about(key, shape, width, most, pieces=(), kind=jnp.bfloat16):
    values = width * jax.random.normal(key, shape, jnp.float32)
    if pieces:
        values = values * block_scale(key, shape, pieces, -0.22, 0.18)
    return jnp.clip(values, -most, most).astype(kind)


def setup_inputs(seed: int = 0) -> dict:
    key_list = jax.random.split(jax.random.key(seed), 5)
    queries = draw_queries(jax.random.fold_in(key_list[4], 71), 0)
    key_states = draw_key_states(jax.random.fold_in(key_list[4], 71), 0)
    value_states = scatter_about(key_list[2], (SEQ, HEADS * HEAD_DIM), 1.0, 6.0, ((0, 128), (1, 4)))
    cotangent = scatter_about(key_list[3], (SEQ, HEADS * HEAD_DIM), 1.0, 6.0, ((0, 512),))
    return {"queries": queries, "key_states": key_states, "value_states": value_states, "cotangent": cotangent}


LOG_TWO = math.log(2.0)
MASKED = -1e+30

def pair_mean(values):
    row_count = values.shape[-2]
    grouped = values.astype(jnp.float32).reshape(values.shape[:-2] + (row_count // 2, 2, values.shape[-1]))
    return (0.5 * (grouped[..., 0, :] + grouped[..., 1, :])).astype(jnp.bfloat16)

def spread_rows(gradients):
    return jnp.repeat(0.5 * gradients, 2, axis=-2)

def attend_block(query_block, key_set, value_set, key_bias, cotangent_block):
    score_scale = 1.0 / math.sqrt(HEAD_DIM)
    flat = HEADS * HEAD_DIM
    query_wide = query_block.astype(jnp.float32).reshape(BLOCK, HEADS, HEAD_DIM)
    key_wide = key_set.astype(jnp.float32).reshape(-1, HEADS, HEAD_DIM)
    value_wide = value_set.astype(jnp.float32).reshape(-1, HEADS, HEAD_DIM)
    cotangent_wide = cotangent_block.astype(jnp.float32).reshape(BLOCK, HEADS, HEAD_DIM)
    scores = jnp.einsum('qhe,khe->hqk', query_wide, key_wide) * score_scale + key_bias
    highest = lax.optimization_barrier(jnp.max(scores, axis=2, keepdims=True))
    raised = jnp.exp(scores - highest)
    weights = raised / lax.optimization_barrier(jnp.sum(raised, axis=2, keepdims=True))
    weights_low = lax.optimization_barrier(weights.astype(jnp.bfloat16)).astype(jnp.float32)
    attended = jnp.einsum('hqk,khe->qhe', weights_low, value_wide).astype(jnp.bfloat16)
    weight_grad = jnp.einsum('qhe,khe->hqk', cotangent_wide, value_wide)
    row_term = lax.optimization_barrier(jnp.sum(weights * weight_grad, axis=2, keepdims=True))
    score_grad = (weights * (weight_grad - row_term) * score_scale).astype(jnp.bfloat16)
    score_grad = lax.optimization_barrier(score_grad).astype(jnp.float32)
    query_grad = jnp.einsum('hqk,khe->qhe', score_grad, key_wide).astype(jnp.bfloat16)
    key_grad = jnp.einsum('hqk,qhe->khe', score_grad, query_wide)
    value_grad = jnp.einsum('hqk,qhe->khe', weights_low, cotangent_wide)
    return (attended.reshape(BLOCK, flat), query_grad.reshape(BLOCK, flat), key_grad.reshape(-1, flat), value_grad.reshape(-1, flat))

def reference(queries, key_states, value_states, cotangent):
    flat = HEADS * HEAD_DIM
    total = BLOCK * N_SEQ
    reach = 2 ** LEVELS - 1
    half_rows = BLOCK // 2
    key_levels = [key_states]
    value_levels = [value_states]
    for level_index in range(1, LEVELS + 1):
        key_levels.append(pair_mean(key_levels[-1]))
        value_levels.append(pair_mean(value_levels[-1]))
    padded_keys = []
    padded_values = []
    for level_index in range(1, LEVELS + 1):
        margin = reach * (BLOCK >> level_index)
        padded_keys.append(jnp.pad(key_levels[level_index], ((margin, margin), (0, 0))))
        padded_values.append(jnp.pad(value_levels[level_index], ((margin, margin), (0, 0))))
    start_grads = tuple((jnp.zeros(padded_level.shape, jnp.float32) for padded_level in padded_keys))

    def step_block(carry, block_index):
        key_sums, value_sums = carry
        start = (block_index * BLOCK).astype(jnp.int32)
        query_block = lax.dynamic_slice_in_dim(queries, start, BLOCK, 0)
        cotangent_block = lax.dynamic_slice_in_dim(cotangent, start, BLOCK, 0)
        key_parts = [lax.dynamic_slice_in_dim(key_states, start, BLOCK, 0)]
        value_parts = [lax.dynamic_slice_in_dim(value_states, start, BLOCK, 0)]
        bias_parts = [jnp.zeros((BLOCK,), jnp.float32)]
        offsets = []
        for level_index in range(1, LEVELS + 1):
            tier_rows = BLOCK >> level_index
            row_block = jnp.arange(half_rows, dtype=jnp.int32) // tier_rows
            lower_first = block_index - 2 ** level_index + 1
            upper_first = block_index + 2 ** (level_index - 1)
            for first_block in (lower_first, upper_first):
                owner_block = first_block + row_block
                valid = (owner_block >= 0) & (owner_block < N_SEQ)
                row_start = ((first_block + reach) * tier_rows).astype(jnp.int32)
                key_parts.append(lax.dynamic_slice_in_dim(padded_keys[level_index - 1], row_start, half_rows, 0))
                value_parts.append(lax.dynamic_slice_in_dim(padded_values[level_index - 1], row_start, half_rows, 0))
                bias_parts.append(jnp.where(valid, level_index * LOG_TWO, MASKED).astype(jnp.float32))
                offsets.append((level_index, row_start))
        attended, query_grad, key_grad, value_grad = attend_block(query_block, jnp.concatenate(key_parts, axis=0), jnp.concatenate(value_parts, axis=0), jnp.concatenate(bias_parts), cotangent_block)
        key_sums = list(key_sums)
        value_sums = list(value_sums)
        for part_number, (level_index, row_start) in enumerate(offsets):
            first_row = BLOCK + part_number * half_rows
            for level_sums, set_grad in ((key_sums, key_grad), (value_sums, value_grad)):
                current = lax.dynamic_slice_in_dim(level_sums[level_index - 1], row_start, half_rows, 0)
                level_sums[level_index - 1] = lax.dynamic_update_slice_in_dim(level_sums[level_index - 1], current + set_grad[first_row:first_row + half_rows], row_start, 0)
        return ((tuple(key_sums), tuple(value_sums)), (attended, query_grad, key_grad[:BLOCK], value_grad[:BLOCK]))
    (key_sums, value_sums), (attended, query_grad, own_key, own_value) = lax.scan(step_block, (start_grads, start_grads), jnp.arange(N_SEQ, dtype=jnp.int32))

    def unfold(level_sums, own_rows):
        carried = None
        for level_index in range(LEVELS, 0, -1):
            tier_rows = BLOCK >> level_index
            core = level_sums[level_index - 1][reach * tier_rows:reach * tier_rows + N_SEQ * tier_rows]
            carried = core if carried is None else core + spread_rows(carried)
        return (own_rows.reshape(total, flat) + spread_rows(carried)).astype(jnp.bfloat16)
    return (attended.reshape(total, flat), query_grad.reshape(total, flat), unfold(key_sums, own_key), unfold(value_sums, own_value))
```

```python
import math

import jax
import jax.numpy as jnp
import numpy as np
from jax import lax
from jax.experimental import pallas as pl
from jax.experimental.pallas import tpu as pltpu
from jax.sharding import PartitionSpec as P

HEAD_DIM = 128
BLOCK = 128
BLOCKS = 128
LOG_TWO = math.log(2.0)
MASKED = -1e30
SCALE = 1.0 / math.sqrt(HEAD_DIM)
VMEM = 56 * 1024 * 1024

SIDE_LEVELS = [1] + [2] * 2 + [3] * 4 + [4] * 8


def _place(matrix, row, col, rows, factor):
    for r in range(rows):
        matrix[row + r, col + r * factor : col + (r + 1) * factor] = 1.0 / factor


def _own_matrix():
    m = np.zeros((240, 256), np.float32)
    row = 0
    for level in range(1, 5):
        for block in range(2):
            rows = BLOCK >> level
            _place(m, row, block * BLOCK, rows, 1 << level)
            row += rows
    return m


def _derive_matrix():
    m = np.zeros((192, 256), np.float32)
    _place(m, 0, 0, 32, 2)
    _place(m, 32, 64, 32, 1)
    _place(m, 64, 96, 16, 2)
    _place(m, 80, 128, 48, 1)
    _place(m, 128, 176, 8, 2)
    _place(m, 136, 192, 56, 1)
    return m


def _second_matrix(right):
    m = np.zeros((96, 224), np.float32)
    ahead, behind = (96, 0) if right else (0, 96)
    near, far = (208, 192) if right else (192, 208)
    _place(m, 0, ahead + 64, 32, 1)
    _place(m, 32, ahead, 16, 4)
    _place(m, 48, near, 16, 1)
    _place(m, 64, far, 16, 1)
    _place(m, 80, behind, 16, 4)
    return m


def _third_matrix(right):
    m = np.zeros((64, 208), np.float32)
    _place(m, 0, 192 if right else 200, 8, 1)
    _place(m, 8, 0, 8, 8)
    _place(m, 16, 64, 8, 4)
    _place(m, 24, 96, 8, 4)
    for i in range(4):
        _place(m, 32 + 8 * i, 128 + 16 * i, 8, 2)
    return m


def _final_matrix():
    own = _own_matrix()
    a1, b1, a2, b2 = own[0:64], own[64:128], own[128:160], own[160:192]
    a3, b3, a4, b4 = own[192:208], own[208:224], own[224:232], own[232:240]
    m = np.zeros((512, 256), np.float32)
    m[0:64], m[64:96] = b1, a2
    m[96:160], m[160:192] = a1, b2
    m[192 + 48 : 192 + 64], m[192 + 64 : 192 + 80] = b3, a3
    m[288 + 48 : 288 + 64], m[288 + 64 : 288 + 80] = a3, b3
    m[384:392] = a4
    m[448:456] = b4
    return m.T.copy()


def _bias_tables():
    side = [(k + 1, lv) for k, lv in enumerate(SIDE_LEVELS) for _ in range(BLOCK >> lv)]
    derived = [(k, lv) for k, lv in zip(range(1, 15), SIDE_LEVELS[1:], strict=True) for _ in range(BLOCK >> lv)]
    a = [(0, 0)] * 128 + [(1, 1)] * 64 + [(1 + k, lv) for k, lv in derived] + [(-k, lv) for k, lv in side]
    b = [(1, 0)] * 128 + [(0, 1)] * 64 + [(-k, lv) for k, lv in derived] + [(1 + k, lv) for k, lv in side]
    table = np.array([a, b], np.int32)
    return table[..., 0], table[..., 1].astype(np.float32) * LOG_TWO


def _bf(m):
    return jnp.asarray(m, jnp.bfloat16)


def _dot(a, b):
    return jnp.dot(a, b, preferred_element_type=jnp.float32)


def _pull(a, b):
    return lax.dot_general(a, b, (((0,), (0,)), ((), ())), preferred_element_type=jnp.float32)


def _outer(a, b):
    return lax.dot_general(a, b, (((1,), (1,)), ((), ())), preferred_element_type=jnp.float32)


def pack_first(core_ref, k_ref, v_ref, own_ref, right_ref, left_ref, one_ref, coarse_ref):
    for part, ref in enumerate((k_ref, v_ref)):
        rows = jnp.concatenate([ref[0], ref[1]], axis=0)
        levels = _dot(own_ref[...], rows).astype(jnp.bfloat16)
        one_ref[part] = levels[0:128]
        right_ref[part] = jnp.concatenate([levels[64:128], levels[128:160]], axis=0)
        left_ref[part] = jnp.concatenate([levels[0:64], levels[160:192]], axis=0)
        coarse_ref[part] = levels[192:240]


def pack_second(l1_ref, r1_ref, coarse_ref, wr_ref, wl_ref, right_ref, left_ref):
    for part in range(2):
        rows = jnp.concatenate([l1_ref[part], r1_ref[part], coarse_ref[part, 0:32]], axis=0)
        right_ref[part] = _dot(wr_ref[...], rows).astype(jnp.bfloat16)
        left_ref[part] = _dot(wl_ref[...], rows).astype(jnp.bfloat16)


def pack_third(l1_ref, r1_ref, l2_ref, r2_ref, coarse_ref, wr_ref, wl_ref, right_ref, left_ref):
    for part in range(2):
        own = coarse_ref[part, 32:48]
        rows = jnp.concatenate([l1_ref[part], l2_ref[part], own], axis=0)
        right_ref[part] = _dot(wr_ref[...], rows).astype(jnp.bfloat16)
        rows = jnp.concatenate([r1_ref[part], r2_ref[part], own], axis=0)
        left_ref[part] = _dot(wl_ref[...], rows).astype(jnp.bfloat16)


def attend(
    core_ref, q_ref, k_ref, v_ref, do_ref, one_ref, l1_ref, l2_ref, l3_ref, r1_ref, r2_ref, r3_ref,
    derive_ref, derive_t_ref, spread_ref, bias_ref,
    o_ref, dq_ref, own_ref, gl_ref, gr_ref, gl3_ref, gr3_ref,
):
    left, right, set_a, set_b = [], [], [], []
    for part, ref in enumerate((k_ref, v_ref)):
        lt = jnp.concatenate([l1_ref[part], l2_ref[part], l3_ref[part]], axis=0)
        rt = jnp.concatenate([r1_ref[part], r2_ref[part], r3_ref[part]], axis=0)
        lt_derived = _dot(derive_ref[...], lt).astype(jnp.bfloat16)
        rt_derived = _dot(derive_ref[...], rt).astype(jnp.bfloat16)
        set_a.append(jnp.concatenate([ref[0], one_ref[part, 64:128], rt_derived, lt], axis=0))
        set_b.append(jnp.concatenate([ref[1], one_ref[part, 0:64], lt_derived, rt], axis=0))
    grads = []
    for block, (keys, values) in enumerate((set_a, set_b)):
        q = q_ref[block]
        do = do_ref[block * BLOCK : (block + 1) * BLOCK]
        scores = _outer(q, keys) * SCALE + bias_ref[block : block + 1]
        highest = jnp.max(scores, axis=1, keepdims=True)
        raised = jnp.exp(scores - highest)
        weights = raised * (1.0 / jnp.sum(raised, axis=1, keepdims=True))
        low = weights.astype(jnp.bfloat16)
        o_ref[block * BLOCK : (block + 1) * BLOCK] = _dot(low, values).astype(jnp.bfloat16)
        weight_grad = _outer(do, values)
        row_term = jnp.sum(weights * weight_grad, axis=1, keepdims=True)
        score_grad = (weights * ((weight_grad - row_term) * SCALE)).astype(jnp.bfloat16)
        dq_ref[block * BLOCK : (block + 1) * BLOCK] = _dot(score_grad, keys).astype(jnp.bfloat16)
        grads.append((_pull(score_grad, q), _pull(low, do)))
    for part in range(2):
        ga, gb = grads[0][part], grads[1][part]
        g_left = ga[384:640] + _dot(derive_t_ref[...], gb[192:384].astype(jnp.bfloat16))
        g_right = gb[384:640] + _dot(derive_t_ref[...], ga[192:384].astype(jnp.bfloat16))
        gl_ref[part] = g_left[0:192]
        gr_ref[part] = g_right[0:192]
        gl3_ref[part] = g_left[192:256].astype(jnp.bfloat16)
        gr3_ref[part] = g_right[192:256].astype(jnp.bfloat16)
        ones = jnp.concatenate([gb[128:192], ga[128:192]], axis=0).astype(jnp.bfloat16)
        own_ref[part] = jnp.concatenate([ga[0:128], gb[0:128]], axis=0) + _dot(spread_ref[...], ones)


def fold_third(gl_ref, gr_ref, fr_ref, fl_ref, w_ref, gl1_ref, gr1_ref, gl2_ref, gr2_ref):
    for part in range(2):
        g = gl_ref[part] + _dot(w_ref[...], fr_ref[part])
        gl1_ref[part] = g[0:96]
        gl2_ref[part] = g[96:192].astype(jnp.bfloat16)
        g = gr_ref[part] + _dot(w_ref[...], fl_ref[part])
        gr1_ref[part] = g[0:96]
        gr2_ref[part] = g[96:192].astype(jnp.bfloat16)


def fold_second(gl1_ref, gr1_ref, fr_ref, fl_ref, w_ref, gl_ref, gr_ref):
    for part in range(2):
        g = _dot(w_ref[...], jnp.concatenate([fr_ref[part], fl_ref[part]], axis=0))
        gl_ref[part] = (gl1_ref[part] + g[0:96]).astype(jnp.bfloat16)
        gr_ref[part] = (gr1_ref[part] + g[96:192]).astype(jnp.bfloat16)


def fold_own(own_ref, f1r, f1l, f2r, f2l, f3r, f3l, w_ref, out_ref):
    for part in range(2):
        rows = jnp.concatenate([f[part] for f in (f1r, f1l, f2r, f2l, f3r, f3l)], axis=0)
        out_ref[part] = (own_ref[part] + _dot(w_ref[...], rows)).astype(jnp.bfloat16)


def _whole(body, outs, *args):
    return pl.pallas_call(
        body,
        out_shape=[jax.ShapeDtypeStruct(s, d) for s, d in outs],
        compiler_params=pltpu.CompilerParams(vmem_limit_bytes=VMEM),
    )(*args)


def local(queries, key_states, value_states, cotangent):
    bf16, f32 = jnp.bfloat16, jnp.float32
    size = lax.axis_size("seq")
    seq = lax.axis_index("seq")
    core = lax.rem(seq, 2)
    half = queries.shape[1] // 2
    heads = half // HEAD_DIM
    n_head = lax.axis_size("head")
    chip_cores = [[2 * i, 2 * i + 1] for i in range(size // 2)]
    chip_groups = [[g * 2 * n_head + m for m in range(2 * n_head)] for g in range(size // 2)]

    def hop(x, chips):
        return lax.ppermute(x, "seq", [(i, (i + 2 * chips) % size) for i in range(size)])

    def both_cores(x):
        return lax.all_gather(x, "seq", axis=0, axis_index_groups=chip_cores)

    split = cotangent.reshape(-1, n_head, 2, half).transpose(2, 1, 0, 3).reshape(2 * n_head, -1, half)
    do = lax.all_to_all(split, ("seq", "head"), 0, 0, axis_index_groups=chip_groups, tiled=True)
    do = do.reshape(2 * BLOCK, half)

    keys, values, quest = both_cores(key_states), both_cores(value_states), both_cores(queries)
    core_arg = core.reshape(1).astype(jnp.int32)

    def rows_out(n, dtype=bf16):
        return ((2, n, half), dtype)

    pick = pl.BlockSpec((2, BLOCK, half), lambda i, c: (0, 0, c[0]))
    whole = lambda n: pl.BlockSpec((2, n, half), lambda i, c: (0, 0, 0))
    p1r, p1l, ones, coarse = pl.pallas_call(
        pack_first,
        out_shape=[jax.ShapeDtypeStruct(*rows_out(n)) for n in (96, 96, 128, 48)],
        grid_spec=pltpu.PrefetchScalarGridSpec(
            num_scalar_prefetch=1,
            grid=(1,),
            in_specs=[pick, pick, pl.BlockSpec((240, 256), lambda i, c: (0, 0))],
            out_specs=[whole(n) for n in (96, 96, 128, 48)],
        ),
        compiler_params=pltpu.CompilerParams(vmem_limit_bytes=VMEM),
    )(core_arg, keys, values, _bf(_own_matrix()))

    l1, r1 = hop(p1r, 1), hop(p1l, -1)
    w2r, w2l = _second_matrix(True), _second_matrix(False)
    p2r, p2l = _whole(pack_second, [rows_out(96)] * 2, l1, r1, coarse, _bf(w2r), _bf(w2l))
    l2, r2 = hop(p2r, 3), hop(p2l, -3)
    w3r, w3l = _third_matrix(True), _third_matrix(False)
    p3r, p3l = _whole(pack_third, [rows_out(64)] * 2, l1, r1, l2, r2, coarse, _bf(w3r), _bf(w3l))
    l3, r3 = hop(p3r, 4), hop(p3l, -4)

    offsets, raise_by = _bias_tables()
    target = seq - core + jnp.asarray(offsets)
    bias = jnp.where((target >= 0) & (target < size), jnp.asarray(raise_by, f32), MASKED).astype(f32)

    def cut(n):
        return pl.BlockSpec((2, n, HEAD_DIM), lambda h, c: (0, 0, h))

    mine = pl.BlockSpec((2, BLOCK, HEAD_DIM), lambda h, c: (0, 0, c[0] * heads + h))
    flat = pl.BlockSpec((2 * BLOCK, HEAD_DIM), lambda h, c: (0, h))
    const = lambda *s: pl.BlockSpec(s, lambda h, c: (0,) * len(s))
    derive = _derive_matrix()
    spread = _own_matrix()[0:128].T.copy()
    attended, dq, own, gl, gr, gl3, gr3 = pl.pallas_call(
        attend,
        out_shape=[jax.ShapeDtypeStruct((2 * BLOCK, half), bf16)] * 2
        + [jax.ShapeDtypeStruct(*rows_out(n, d)) for n, d in ((256, f32), (192, f32), (192, f32), (64, bf16), (64, bf16))],
        grid_spec=pltpu.PrefetchScalarGridSpec(
            num_scalar_prefetch=1,
            grid=(heads,),
            in_specs=[mine, mine, mine, flat, cut(128)]
            + [cut(96), cut(96), cut(64)] * 2
            + [const(192, 256), const(256, 192), const(256, 128), const(2, 640)],
            out_specs=[flat, flat, cut(256), cut(192), cut(192), cut(64), cut(64)],
        ),
        compiler_params=pltpu.CompilerParams(vmem_limit_bytes=VMEM),
    )(
        core_arg, quest, keys, values, do, ones, l1, l2, l3, r1, r2, r3,
        _bf(derive), _bf(derive.T.copy()), _bf(spread), bias,
    )

    f3l, f3r = hop(gr3, 4), hop(gl3, -4)
    w3t = w3r[:, 0:192].T.copy()
    gl1, gr1, gl2, gr2 = _whole(
        fold_third, [rows_out(96, f32)] * 2 + [rows_out(96)] * 2, gl, gr, f3r, f3l, _bf(w3t)
    )
    f2l, f2r = hop(gr2, 3), hop(gl2, -3)
    w2t = np.concatenate([w2r[:, 0:192], w2l[:, 0:192]], axis=0).T.copy()
    s1l, s1r = _whole(fold_second, [rows_out(96)] * 2, gl1, gr1, f2r, f2l, _bf(w2t))
    f1l, f1r = hop(s1r, 1), hop(s1l, -1)
    (own,) = _whole(fold_own, [rows_out(256)], own, f1r, f1l, f2r, f2l, f3r, f3l, _bf(_final_matrix()))

    out = lax.all_to_all(
        attended.reshape(2 * n_head, -1, half), ("seq", "head"), 0, 0, axis_index_groups=chip_groups, tiled=True
    )
    out = out.reshape(2, n_head, -1, half).transpose(2, 1, 0, 3).reshape(-1, n_head * 2 * half)

    grads = jnp.concatenate([own, dq[None]], axis=0).reshape(3, 2, BLOCK, half)
    keep = lax.dynamic_index_in_dim(grads, core, 1, keepdims=False)
    give = lax.dynamic_index_in_dim(grads, 1 - core, 1, keepdims=False)
    take = lax.ppermute(give, "seq", [(i, i ^ 1) for i in range(size)])
    low = jnp.where(core == 0, keep, take)
    high = jnp.where(core == 0, take, keep)
    full = jnp.concatenate([low, high], axis=2)
    return (out, full[2], full[0], full[1])


def solution(mesh):
    placed = (P("seq", "head"), P("seq", "head"), P("seq", "head"), P(("seq", "head"), None))
    return jax.shard_map(
        local,
        mesh=mesh,
        in_specs=placed,
        out_specs=(P(("seq", "head"), None), P("seq", "head"), P("seq", "head"), P("seq", "head")),
        check_vma=False,
    )
```

```python
import math

import jax
import jax.numpy as jnp
import numpy as np
from jax import lax
from jax.experimental import pallas as pl
from jax.experimental.pallas import tpu as pltpu
from jax.sharding import PartitionSpec as P

HEAD_DIM = 128
BLOCK = 128
BLOCKS = 128
LOG_TWO = math.log(2.0)
MASKED = -1e30
SCALE = 1.0 / math.sqrt(HEAD_DIM)
VMEM = 10 * 1024 * 1024
HALF = 512

SIDE_LEVELS = [0] + [1] + [2] * 2 + [3] * 4 + [4] * 8
VIEW = {1: [1, 2, 7, 8, 13, 14], 2: [3, 4, 9, 10, 15], 3: [5, 6], 6: [11, 12]}
VIEW_BLOCKS = VIEW[1] + VIEW[2] + VIEW[3] + VIEW[6]
FAR_BLOCKS = VIEW[3] + VIEW[6]
LEVEL_ORDER = [(level, block) for level in (1, 2, 3, 4) for block in "PO"]


def _rows(level):
    return BLOCK >> level


def _starts(blocks, level_of):
    starts, row = {}, 0
    for k in blocks:
        starts[k] = row
        row += _rows(level_of(k))
    return starts, row


def _finest(k):
    return SIDE_LEVELS[k]


def _pool(matrix, row, col, rows, factor):
    for r in range(rows):
        matrix[row + r, col + r * factor : col + (r + 1) * factor] = 1.0 / factor


def _own_matrix():
    m = np.zeros((240, 256), np.float32)
    row = 0
    for level, block in LEVEL_ORDER:
        _pool(m, row, 0 if block == "P" else BLOCK, _rows(level), 1 << level)
        row += _rows(level)
    return m


def _own_rows(level, block):
    row = 0
    for entry in LEVEL_ORDER:
        if entry == (level, block):
            return row, row + _rows(level)
        row += _rows(entry[0])
    raise KeyError


def _own_sent(distance):
    return [(_finest(2 * distance - 1), "O"), (_finest(2 * distance), "P")]


def _pass_matrix():
    cols, width = _starts(FAR_BLOCKS, _finest)
    sent = [(k, 1) for k in VIEW[1][2:]] + [(k, 2) for k in VIEW[2][2:]]
    m = np.zeros((sum(_rows(_finest(k)) for k, _ in sent), width), np.float32)
    row = 0
    for k, distance in sent:
        held = k - 2 * distance
        _pool(m, row, cols[held], _rows(_finest(k)), 1 << (_finest(k) - _finest(held)))
        row += _rows(_finest(k))
    return m


def _derive_matrix():
    cols, width = _starts(VIEW_BLOCKS, _finest)
    blocks = [k for k in VIEW_BLOCKS if k < 15]
    rows, height = _starts(blocks, lambda k: SIDE_LEVELS[k + 1])
    m = np.zeros((height, width), np.float32)
    for k in blocks:
        level = SIDE_LEVELS[k + 1]
        _pool(m, rows[k], cols[k], _rows(level), 1 << (level - _finest(k)))
    return m


def _final_matrix():
    own = _own_matrix()
    m = np.zeros((256, 256), np.float32)
    row = 0
    for distance, blocks in VIEW.items():
        start = row
        for level, block in _own_sent(distance):
            first, last = _own_rows(level, block)
            m[start : start + last - first] = own[first:last]
            start += last - first
        row += sum(_rows(_finest(k)) for k in blocks)
    return m.T.copy()


def _bias_tables():
    derived = [(k, SIDE_LEVELS[k + 1]) for k in VIEW_BLOCKS if k < 15]
    direct = [(k, _finest(k)) for k in VIEW_BLOCKS]
    p = [(0, 0, 128), (-1, 1, 64)] + [(k, lv, _rows(lv)) for k, lv in direct] + [(-1 - k, lv, _rows(lv)) for k, lv in derived]
    o = [(-1, 0, 128), (0, 1, 64)] + [(-1 - k, lv, _rows(lv)) for k, lv in direct] + [(k, lv, _rows(lv)) for k, lv in derived]
    table = np.array([[(off, lv) for off, lv, n in part for _ in range(n)] for part in (p, o)], np.int32)
    return table[..., 0], table[..., 1].astype(np.float32) * LOG_TWO


def _bf(m):
    return jnp.asarray(m, jnp.bfloat16)


def _dot(a, b):
    return jnp.dot(a, b, preferred_element_type=jnp.float32)


def _pull(a, b):
    return lax.dot_general(a, b, (((0,), (0,)), ((), ())), preferred_element_type=jnp.float32)


def _outer(a, b):
    return lax.dot_general(a, b, (((1,), (1,)), ((), ())), preferred_element_type=jnp.float32)


def _wide(*parts):
    return jnp.concatenate([p.astype(jnp.float32) for p in parts], axis=0)


def _half(core):
    return pl.ds(pl.multiple_of(core * HALF, HALF), HALF)


def pack_own(core_ref, k_ref, v_ref, own_ref, three_ref, six_ref, one_own_ref, two_own_ref, ones_ref):
    core = core_ref[0]
    for part, ref in enumerate((k_ref, v_ref)):
        levels = _dot(own_ref[...], jnp.concatenate([ref[core], ref[1 - core]], axis=0))
        for out, distance in ((three_ref, 3), (six_ref, 6), (one_own_ref, 1), (two_own_ref, 2)):
            spans = [_own_rows(level, block) for level, block in _own_sent(distance)]
            out[part] = jnp.concatenate([levels[a:b] for a, b in spans], axis=0).astype(jnp.bfloat16)
        one_own = jnp.concatenate([ref[core, :, _half(core)], ref[1 - core, :, _half(core)]], axis=0)
        ones_ref[part] = _dot(own_ref[0:128], one_own).astype(jnp.bfloat16)


def pack_on(three_ref, six_ref, one_own_ref, two_own_ref, w_ref, one_ref, two_ref):
    for part in range(2):
        on = _dot(w_ref[...], jnp.concatenate([three_ref[part], six_ref[part]], axis=0))
        one_ref[part] = _wide(one_own_ref[part], on[0:40]).astype(jnp.bfloat16)
        two_ref[part] = _wide(two_own_ref[part], on[40:64]).astype(jnp.bfloat16)


def join_view(core_ref, one_ref, two_ref, three_ref, six_ref, mine_ref, give_ref):
    core = core_ref[0]
    for out, lanes in ((mine_ref, _half(core)), (give_ref, _half(1 - core))):
        for part in range(2):
            near = _wide(one_ref[part, :, lanes], two_ref[part, :, lanes]).astype(jnp.bfloat16)
            out[part, 0:208] = near
            out[part, 208:240] = three_ref[part, :, lanes]
            out[part, 240:256] = six_ref[part, :, lanes]


def attend(
    core_ref, q_ref, k_ref, v_ref, do_ref, ones_ref, x_ref, y_ref, derive_ref, derive_t_ref, spread_ref, bias_ref,
    o_ref, dqp_ref, dqo_ref, gp_ref, go_ref, gx_ref, gy_ref,
):
    core = core_ref[0]
    lanes = pl.ds(pl.multiple_of(pl.program_id(0) * HEAD_DIM, HEAD_DIM), HEAD_DIM)
    sets_p, sets_o = [], []
    for part, ref in enumerate((k_ref, v_ref)):
        x, y = x_ref[part, :, lanes], y_ref[part, :, lanes]
        x_derived = _dot(derive_ref[...], x).astype(jnp.bfloat16)
        y_derived = _dot(derive_ref[...], y).astype(jnp.bfloat16)
        sets_p.append(jnp.concatenate([ref[core], ones_ref[part, 64:128, lanes], x, y_derived], axis=0))
        sets_o.append(jnp.concatenate([ref[1 - core], ones_ref[part, 0:64, lanes], y, x_derived], axis=0))
    grads = []
    for block, (keys, values) in enumerate((sets_p, sets_o)):
        place = core if block == 0 else 1 - core
        here = pl.ds(pl.multiple_of(place * BLOCK, BLOCK), BLOCK)
        q = q_ref[place]
        do = do_ref[here, lanes]
        scores = _outer(q, keys) * SCALE + bias_ref[block : block + 1]
        highest = jnp.max(scores, axis=1, keepdims=True)
        raised = jnp.exp(scores - highest)
        weights = raised * (1.0 / jnp.sum(raised, axis=1, keepdims=True))
        low = weights.astype(jnp.bfloat16)
        o_ref[here, lanes] = _dot(low, values).astype(jnp.bfloat16)
        weight_grad = _outer(do, values)
        row_term = jnp.sum(weights * weight_grad, axis=1, keepdims=True)
        score_grad = (weights * ((weight_grad - row_term) * SCALE)).astype(jnp.bfloat16)
        dq_ref = dqp_ref if block == 0 else dqo_ref
        dq_ref[:, lanes] = _dot(score_grad, keys).astype(jnp.bfloat16)
        grads.append((_pull(score_grad, q), _pull(low, do)))
    for part in range(2):
        gp, go = grads[0][part], grads[1][part]
        gx = gp[192:448] + _dot(derive_t_ref[...], go[448:640].astype(jnp.bfloat16))
        gy = go[192:448] + _dot(derive_t_ref[...], gp[448:640].astype(jnp.bfloat16))
        gx_ref[part, :, lanes] = gx.astype(jnp.bfloat16)
        gy_ref[part, :, lanes] = gy.astype(jnp.bfloat16)
        gp_ref[part, :, lanes] = gp[0:128] + _dot(spread_ref[...], go[128:192].astype(jnp.bfloat16))
        go_ref[part, :, lanes] = go[0:128] + _dot(spread_ref[...], gp[128:192].astype(jnp.bfloat16))


def split_view(core_ref, mine_ref, take_ref, one_ref, two_ref, far_ref):
    core = core_ref[0]
    for src, lanes in ((mine_ref, _half(core)), (take_ref, _half(1 - core))):
        for part in range(2):
            near = src[part, 0:208].astype(jnp.float32)
            one_ref[part, :, lanes] = near[0:136].astype(jnp.bfloat16)
            two_ref[part, :, lanes] = near[136:208].astype(jnp.bfloat16)
            far_ref[part, :, lanes] = src[part, 208:256]


def fold_on(far_ref, one_ref, two_ref, w_ref, three_ref, six_ref):
    for part in range(2):
        back = _wide(one_ref[part], two_ref[part])
        on = jnp.concatenate([back[96:136], back[184:208]], axis=0).astype(jnp.bfloat16)
        far = far_ref[part].astype(jnp.float32) + _dot(w_ref[...], on)
        three_ref[part] = far[0:32].astype(jnp.bfloat16)
        six_ref[part] = far[32:48].astype(jnp.bfloat16)


def fold_own(core_ref, one_ref, two_ref, three_ref, six_ref, gp_ref, go_ref, w_ref, keep_ref, give_ref):
    lanes = _half(core_ref[0])
    for part in range(2):
        near = _wide(one_ref[part], two_ref[part]).astype(jnp.bfloat16)
        total = _dot(w_ref[...], jnp.concatenate([near, three_ref[part], six_ref[part]], axis=0))
        keep_ref[part] = total[0:BLOCK]
        keep_ref[part, :, lanes] += gp_ref[part]
        give_ref[part] = total[BLOCK:].astype(jnp.bfloat16)
        give_ref[part, :, lanes] = (give_ref[part, :, lanes].astype(jnp.float32) + go_ref[part]).astype(jnp.bfloat16)


def finish(keep_ref, take_ref, k_ref, v_ref):
    for part, ref in enumerate((k_ref, v_ref)):
        ref[...] = (keep_ref[part] + take_ref[part].astype(jnp.float32)).astype(jnp.bfloat16)


VMEM_SPEC = pl.BlockSpec(memory_space=pltpu.VMEM)
SMEM_SPEC = pl.BlockSpec(memory_space=pltpu.SMEM)


def _whole(body, outs, *args, scalars=0):
    return pl.pallas_call(
        body,
        out_shape=[jax.ShapeDtypeStruct(s, d) for s, d in outs],
        in_specs=[SMEM_SPEC] * scalars + [VMEM_SPEC] * (len(args) - scalars),
        out_specs=[VMEM_SPEC] * len(outs),
        compiler_params=pltpu.CompilerParams(vmem_limit_bytes=VMEM),
    )(*args)


def local(queries, key_states, value_states, cotangent):
    bf16, f32 = jnp.bfloat16, jnp.float32
    tie = lax.optimization_barrier
    size = lax.axis_size("seq")
    seq = lax.axis_index("seq")
    core = lax.rem(seq, 2)
    width = queries.shape[1]
    half = width // 2
    heads = half // HEAD_DIM
    n_head = lax.axis_size("head")
    chip_cores = [[2 * i, 2 * i + 1] for i in range(size // 2)]
    chip_groups = [[g * 2 * n_head + m for m in range(2 * n_head)] for g in range(size // 2)]

    def hop(x, chips):
        return lax.ppermute(x, "seq", [(i, (i + (2 - 4 * (i % 2)) * chips) % size) for i in range(size)])

    def swap(x):
        return lax.ppermute(x, "seq", [(i, i ^ 1) for i in range(size)])

    def both_cores(x):
        return lax.all_gather(x, "seq", axis=0, axis_index_groups=chip_cores)

    def full(n, dtype=bf16):
        return ((2, n, width), dtype)

    def part(n, dtype=bf16):
        return ((2, n, half), dtype)

    keys, values = both_cores(key_states), both_cores(value_states)
    core_arg = core.reshape(1).astype(jnp.int32)

    t3, t6, own1, own2, ones = _whole(
        pack_own, [full(32), full(16), full(96), full(48), part(128)],
        core_arg, keys, values, _bf(_own_matrix()), scalars=1,
    )
    t3, t6, late_queries = tie((t3, t6, queries))
    r3, r6 = hop(t3, 3), hop(t6, 6)
    quest = both_cores(late_queries)
    r3, r6, quest, late_cotangent = tie((r3, r6, quest, cotangent))

    t1, t2 = _whole(pack_on, [full(136), full(72)], r3, r6, own1, own2, _bf(_pass_matrix()))
    t1, t2, late_cotangent = tie((t1, t2, late_cotangent))
    r2, r1 = hop(t2, 2), hop(t1, 1)
    split = late_cotangent.reshape(-1, n_head, 2, half).transpose(2, 1, 0, 3).reshape(2 * n_head, -1, half)
    do = lax.all_to_all(split, ("seq", "head"), 0, 0, axis_index_groups=chip_groups, tiled=True)
    do = do.reshape(2 * BLOCK, half)
    r1, r2, do = tie((r1, r2, do))
    mine, give = _whole(join_view, [part(256)] * 2, core_arg, r1, r2, r3, r6, scalars=1)
    other = swap(give)

    offsets, raise_by = _bias_tables()
    target = seq + (2 * core - 1) * jnp.asarray(offsets)
    bias = jnp.where((target >= 0) & (target < size), jnp.asarray(raise_by, f32), MASKED).astype(f32)

    pick = pl.BlockSpec((2, BLOCK, HEAD_DIM), lambda h, c: (0, 0, c[0] * heads + h))
    derive = _derive_matrix()
    spread = _own_matrix()[0:64, 0:BLOCK].T.copy()
    outs = [((2 * BLOCK, half), bf16)] + [((BLOCK, half), bf16)] * 2 + [part(BLOCK, f32)] * 2 + [part(256)] * 2
    attended, dq_mine, dq_give, gp, go, gx, gy = pl.pallas_call(
        attend,
        out_shape=[jax.ShapeDtypeStruct(s, d) for s, d in outs],
        grid_spec=pltpu.PrefetchScalarGridSpec(
            num_scalar_prefetch=1,
            grid=(heads,),
            in_specs=[pick] * 3 + [VMEM_SPEC] * 8,
            out_specs=[VMEM_SPEC] * len(outs),
        ),
        compiler_params=pltpu.CompilerParams(vmem_limit_bytes=VMEM),
    )(core_arg, quest, keys, values, do, ones, mine, other, _bf(derive), _bf(derive.T.copy()), _bf(spread), bias)

    u1, u2, far = _whole(split_view, [full(136), full(72), full(48)], core_arg, gx, swap(gy), scalars=1)
    u1, u2, attended, dq_give = tie((u1, u2, attended, dq_give))
    v2, v1 = hop(u2, -2), hop(u1, -1)

    out = lax.all_to_all(
        attended.reshape(2 * n_head, -1, half), ("seq", "head"), 0, 0, axis_index_groups=chip_groups, tiled=True
    )
    v1, v2, out, dq_give = tie((v1, v2, out, dq_give))

    u3, u6 = _whole(fold_on, [full(32), full(16)], far, v1, v2, _bf(_pass_matrix().T.copy()))
    u3, u6, out, dq_give = tie((u3, u6, out, dq_give))
    v3, v6 = hop(u3, -3), hop(u6, -6)
    out = out.reshape(2, n_head, -1, half).transpose(2, 1, 0, 3).reshape(-1, n_head * width)
    dq_take = swap(dq_give)
    query_gradient = jnp.concatenate(
        [jnp.where(core == 0, dq_mine, dq_take), jnp.where(core == 0, dq_take, dq_mine)], axis=1
    )
    v3, v6, out, query_gradient = tie((v3, v6, out, query_gradient))
    keep, back = _whole(
        fold_own, [full(BLOCK, f32), full(BLOCK)], core_arg, v1, v2, v3, v6, gp, go, _bf(_final_matrix()), scalars=1
    )
    key_gradient, value_gradient = pl.pallas_call(
        finish,
        out_shape=[jax.ShapeDtypeStruct((BLOCK, width), bf16)] * 2,
        in_specs=[VMEM_SPEC] * 2,
        compiler_params=pltpu.CompilerParams(vmem_limit_bytes=VMEM),
    )(keep, swap(back))
    return (out, query_gradient, key_gradient, value_gradient)


def solution(mesh):
    placed = (P("seq", "head"), P("seq", "head"), P("seq", "head"), P(("seq", "head"), None))
    return jax.shard_map(
        local,
        mesh=mesh,
        in_specs=placed,
        out_specs=(P(("seq", "head"), None), P("seq", "head"), P("seq", "head"), P("seq", "head")),
        check_vma=False,
    )
```

```python
import math

import jax
import jax.numpy as jnp
import numpy as np
from jax import lax
from jax.experimental import pallas as pl
from jax.experimental.pallas import tpu as pltpu
from jax.sharding import PartitionSpec as P

HEAD_DIM = 128
BLOCK = 128
BLOCKS = 128
LOG_TWO = math.log(2.0)
MASKED = -1e30
SCALE = 1.0 / math.sqrt(HEAD_DIM)
VMEM = 4 * 1024 * 1024
WIDE_VMEM = 52 * 1024 * 1024
HALF = 512

SIDE_LEVELS = [0] + [1] + [2] * 2 + [3] * 4 + [4] * 8
VIEW = {1: [1, 2, 7, 8, 13, 14], 2: [3, 4, 9, 10, 15], 3: [5, 6], 6: [11, 12]}
VIEW_BLOCKS = VIEW[1] + VIEW[2] + VIEW[3] + VIEW[6]
FAR_BLOCKS = VIEW[3] + VIEW[6]
LEVEL_ORDER = [(level, block) for level in (1, 2, 3, 4) for block in "PO"]


def _rows(level):
    return BLOCK >> level


def _starts(blocks, level_of):
    starts, row = {}, 0
    for k in blocks:
        starts[k] = row
        row += _rows(level_of(k))
    return starts, row


def _finest(k):
    return SIDE_LEVELS[k]


def _pool(matrix, row, col, rows, factor):
    for r in range(rows):
        matrix[row + r, col + r * factor : col + (r + 1) * factor] = 1.0 / factor


def _own_matrix():
    m = np.zeros((240, 256), np.float32)
    row = 0
    for level, block in LEVEL_ORDER:
        _pool(m, row, 0 if block == "P" else BLOCK, _rows(level), 1 << level)
        row += _rows(level)
    return m


def _own_rows(level, block):
    row = 0
    for entry in LEVEL_ORDER:
        if entry == (level, block):
            return row, row + _rows(level)
        row += _rows(entry[0])
    raise KeyError


def _own_sent(distance):
    return [(_finest(2 * distance - 1), "O"), (_finest(2 * distance), "P")]


def _pass_matrix():
    cols, width = _starts(FAR_BLOCKS, _finest)
    sent = [(k, 1) for k in VIEW[1][2:]] + [(k, 2) for k in VIEW[2][2:]]
    m = np.zeros((sum(_rows(_finest(k)) for k, _ in sent), width), np.float32)
    row = 0
    for k, distance in sent:
        held = k - 2 * distance
        _pool(m, row, cols[held], _rows(_finest(k)), 1 << (_finest(k) - _finest(held)))
        row += _rows(_finest(k))
    return m


def _derive_matrix():
    cols, width = _starts(VIEW_BLOCKS, _finest)
    blocks = [k for k in VIEW_BLOCKS if k < 15]
    rows, height = _starts(blocks, lambda k: SIDE_LEVELS[k + 1])
    m = np.zeros((height, width), np.float32)
    for k in blocks:
        level = SIDE_LEVELS[k + 1]
        _pool(m, rows[k], cols[k], _rows(level), 1 << (level - _finest(k)))
    return m


def _final_matrix():
    own = _own_matrix()
    m = np.zeros((256, 256), np.float32)
    row = 0
    for distance, blocks in VIEW.items():
        start = row
        for level, block in _own_sent(distance):
            first, last = _own_rows(level, block)
            m[start : start + last - first] = own[first:last]
            start += last - first
        row += sum(_rows(_finest(k)) for k in blocks)
    return m.T.copy()


def _bias_tables():
    derived = [(k, SIDE_LEVELS[k + 1]) for k in VIEW_BLOCKS if k < 15]
    direct = [(k, _finest(k)) for k in VIEW_BLOCKS]
    p = [(0, 0, 128), (-1, 1, 64)] + [(k, lv, _rows(lv)) for k, lv in direct] + [(-1 - k, lv, _rows(lv)) for k, lv in derived]
    o = [(-1, 0, 128), (0, 1, 64)] + [(-1 - k, lv, _rows(lv)) for k, lv in direct] + [(k, lv, _rows(lv)) for k, lv in derived]
    table = np.array([[(off, lv) for off, lv, n in part for _ in range(n)] for part in (p, o)], np.int32)
    return table[..., 0], table[..., 1].astype(np.float32) * LOG_TWO


def _bf(m):
    return jnp.asarray(m, jnp.bfloat16)


def _dot(a, b):
    return jnp.dot(a, b, preferred_element_type=jnp.float32)


def _pull(a, b):
    return lax.dot_general(a, b, (((0,), (0,)), ((), ())), preferred_element_type=jnp.float32)


def _outer(a, b):
    return lax.dot_general(a, b, (((1,), (1,)), ((), ())), preferred_element_type=jnp.float32)


def _wide(*parts):
    return jnp.concatenate([p.astype(jnp.float32) for p in parts], axis=0)


def _half(core):
    return pl.ds(pl.multiple_of(core * HALF, HALF), HALF)


def pack_own(core_ref, k_ref, v_ref, own_ref, three_ref, six_ref, one_own_ref, two_own_ref, ones_ref):
    core = core_ref[0]
    for part, ref in enumerate((k_ref, v_ref)):
        levels = _dot(own_ref[...], jnp.concatenate([ref[core], ref[1 - core]], axis=0))
        for out, distance in ((three_ref, 3), (six_ref, 6), (one_own_ref, 1), (two_own_ref, 2)):
            spans = [_own_rows(level, block) for level, block in _own_sent(distance)]
            out[part] = jnp.concatenate([levels[a:b] for a, b in spans], axis=0).astype(jnp.bfloat16)
        one_own = jnp.concatenate([ref[core, :, _half(core)], ref[1 - core, :, _half(core)]], axis=0)
        ones_ref[part] = _dot(own_ref[0:128], one_own).astype(jnp.bfloat16)


def pack_on(three_ref, six_ref, one_own_ref, two_own_ref, w_ref, one_ref, two_ref):
    for part in range(2):
        on = _dot(w_ref[...], jnp.concatenate([three_ref[part], six_ref[part]], axis=0))
        one_ref[part] = _wide(one_own_ref[part], on[0:40]).astype(jnp.bfloat16)
        two_ref[part] = _wide(two_own_ref[part], on[40:64]).astype(jnp.bfloat16)


def join_view(core_ref, one_ref, two_ref, three_ref, six_ref, q_ref, mine_ref, give_ref):
    core = core_ref[0]
    for out, lanes in ((mine_ref, _half(core)), (give_ref, _half(1 - core))):
        for part in range(2):
            near = _wide(one_ref[part, :, lanes], two_ref[part, :, lanes]).astype(jnp.bfloat16)
            out[2 * part] = near[0:128]
            out[2 * part + 1, 0:80] = near[128:208]
            out[2 * part + 1, 80:112] = three_ref[part, :, lanes]
            out[2 * part + 1, 112:128] = six_ref[part, :, lanes]
        out[4] = q_ref[:, lanes]


def attend(
    core_ref, k_ref, v_ref, do_ref, ones_ref, x_ref, y_ref, derive_ref, derive_t_ref, spread_ref, bias_ref,
    o_ref, dq_ref, gp_ref, go_ref, gx_ref, gy_ref,
):
    core = core_ref[0]
    lanes = pl.ds(pl.multiple_of(pl.program_id(0) * HEAD_DIM, HEAD_DIM), HEAD_DIM)
    sets_p, sets_o = [], []
    for part, ref in enumerate((k_ref, v_ref)):
        x = jnp.concatenate([x_ref[2 * part], x_ref[2 * part + 1]], axis=0)
        y = jnp.concatenate([y_ref[2 * part], y_ref[2 * part + 1]], axis=0)
        x_derived = _dot(derive_ref[...], x).astype(jnp.bfloat16)
        y_derived = _dot(derive_ref[...], y).astype(jnp.bfloat16)
        sets_p.append(jnp.concatenate([ref[core], ones_ref[part, 64:128], x, y_derived], axis=0))
        sets_o.append(jnp.concatenate([ref[1 - core], ones_ref[part, 0:64], y, x_derived], axis=0))
    grads = []
    for block, (keys, values) in enumerate((sets_p, sets_o)):
        place = core if block == 0 else 1 - core
        here = pl.ds(pl.multiple_of(place * BLOCK, BLOCK), BLOCK)
        q = (x_ref, y_ref)[block][4]
        do = do_ref[here]
        scores = _outer(q, keys) * SCALE + bias_ref[block : block + 1]
        highest = jnp.max(scores, axis=1, keepdims=True)
        raised = jnp.exp(scores - highest)
        weights = raised * (1.0 / jnp.sum(raised, axis=1, keepdims=True))
        low = weights.astype(jnp.bfloat16)
        o_ref[here, lanes] = _dot(low, values).astype(jnp.bfloat16)
        weight_grad = _outer(do, values)
        row_term = jnp.sum(weights * weight_grad, axis=1, keepdims=True)
        score_grad = (weights * ((weight_grad - row_term) * SCALE)).astype(jnp.bfloat16)
        dq = _dot(score_grad, keys).astype(jnp.bfloat16)
        if block == 0:
            dq_ref[:, lanes] = dq
        else:
            gy_ref[4, :, lanes] = dq
        grads.append((_pull(score_grad, q), _pull(low, do)))
    for part in range(2):
        gp, go = grads[0][part], grads[1][part]
        gx = gp[192:448] + _dot(derive_t_ref[...], go[448:640].astype(jnp.bfloat16))
        gy = go[192:448] + _dot(derive_t_ref[...], gp[448:640].astype(jnp.bfloat16))
        for g, ref in ((gx, gx_ref), (gy, gy_ref)):
            ref[2 * part, :, lanes] = g[0:128].astype(jnp.bfloat16)
            ref[2 * part + 1, :, lanes] = g[128:256].astype(jnp.bfloat16)
        gp_ref[part, :, lanes] = gp[0:128] + _dot(spread_ref[...], go[128:192].astype(jnp.bfloat16))
        go_ref[part, :, lanes] = go[0:128] + _dot(spread_ref[...], gp[128:192].astype(jnp.bfloat16))


def split_view(core_ref, mine_ref, take_ref, one_ref, two_ref, far_ref):
    core = core_ref[0]
    for src, lanes in ((mine_ref, _half(core)), (take_ref, _half(1 - core))):
        for part in range(2):
            near = _wide(src[2 * part], src[2 * part + 1, 0:80])
            one_ref[part, :, lanes] = near[0:136].astype(jnp.bfloat16)
            two_ref[part, :, lanes] = near[136:208].astype(jnp.bfloat16)
            far_ref[part, :, lanes] = src[2 * part + 1, 80:128]


def fold_on(far_ref, one_ref, two_ref, w_ref, three_ref, six_ref):
    for part in range(2):
        back = _wide(one_ref[part], two_ref[part])
        on = jnp.concatenate([back[96:136], back[184:208]], axis=0).astype(jnp.bfloat16)
        far = far_ref[part].astype(jnp.float32) + _dot(w_ref[...], on)
        three_ref[part] = far[0:32].astype(jnp.bfloat16)
        six_ref[part] = far[32:48].astype(jnp.bfloat16)


def fold_own(core_ref, one_ref, two_ref, three_ref, six_ref, gp_ref, go_ref, w_ref, keep_ref, give_ref):
    lanes = _half(core_ref[0])
    for part in range(2):
        near = _wide(one_ref[part], two_ref[part]).astype(jnp.bfloat16)
        total = _dot(w_ref[...], jnp.concatenate([near, three_ref[part], six_ref[part]], axis=0))
        keep_ref[part] = total[0:BLOCK]
        keep_ref[part, :, lanes] += gp_ref[part]
        give_ref[part] = total[BLOCK:].astype(jnp.bfloat16)
        give_ref[part, :, lanes] = (give_ref[part, :, lanes].astype(jnp.float32) + go_ref[part]).astype(jnp.bfloat16)


def finish(keep_ref, take_ref, k_ref, v_ref):
    for part, ref in enumerate((k_ref, v_ref)):
        ref[...] = (keep_ref[part] + take_ref[part].astype(jnp.float32)).astype(jnp.bfloat16)


VMEM_SPEC = pl.BlockSpec(memory_space=pltpu.VMEM)
SMEM_SPEC = pl.BlockSpec(memory_space=pltpu.SMEM)


def _whole(body, outs, *args, scalars=0):
    return pl.pallas_call(
        body,
        out_shape=[jax.ShapeDtypeStruct(s, d) for s, d in outs],
        in_specs=[SMEM_SPEC] * scalars + [VMEM_SPEC] * (len(args) - scalars),
        out_specs=[VMEM_SPEC] * len(outs),
        compiler_params=pltpu.CompilerParams(vmem_limit_bytes=VMEM),
    )(*args)


def local(queries, key_states, value_states, cotangent):
    bf16, f32 = jnp.bfloat16, jnp.float32
    tie = lax.optimization_barrier
    size = lax.axis_size("seq")
    seq = lax.axis_index("seq")
    core = lax.rem(seq, 2)
    width = queries.shape[1]
    half = width // 2
    heads = half // HEAD_DIM
    n_head = lax.axis_size("head")
    chip_cores = [[2 * i, 2 * i + 1] for i in range(size // 2)]
    chip_groups = [[g * 2 * n_head + m for m in range(2 * n_head)] for g in range(size // 2)]

    def hop(x, chips):
        pairs = [(i, i + (2 - 4 * (i % 2)) * chips) for i in range(size)]
        return lax.ppermute(x, "seq", [(i, j) for i, j in pairs if 0 <= j < size])

    def swap(x):
        return lax.ppermute(x, "seq", [(i, i ^ 1) for i in range(size)])

    def both_cores(x):
        return lax.all_gather(x, "seq", axis=0, axis_index_groups=chip_cores)

    def full(n, dtype=bf16):
        return ((2, n, width), dtype)

    view = ((5, BLOCK, half), bf16)

    def part(n, dtype=bf16):
        return ((2, n, half), dtype)

    keys, values = both_cores(key_states), both_cores(value_states)
    core_arg = core.reshape(1).astype(jnp.int32)

    t3, t6, own1, own2, ones = _whole(
        pack_own, [full(32), full(16), full(96), full(48), part(128)],
        core_arg, keys, values, _bf(_own_matrix()), scalars=1,
    )
    r3, r6 = hop(t3, 3), hop(t6, 6)
    r3, r6, late_cotangent = tie((r3, r6, cotangent))

    t1, t2 = _whole(pack_on, [full(136), full(72)], r3, r6, own1, own2, _bf(_pass_matrix()))
    t1, t2, late_cotangent = tie((t1, t2, late_cotangent))
    r2, r1 = hop(t2, 2), hop(t1, 1)
    split = late_cotangent.reshape(-1, n_head, 2, half).transpose(2, 1, 0, 3).reshape(2 * n_head, -1, half)
    do = lax.all_to_all(split, ("seq", "head"), 0, 0, axis_index_groups=chip_groups, tiled=True)
    do = do.reshape(2 * BLOCK, half)
    r1, r2, do = tie((r1, r2, do))
    mine, give = _whole(join_view, [view] * 2, core_arg, r1, r2, r3, r6, queries, scalars=1)
    other = swap(give)

    offsets, raise_by = _bias_tables()
    target = seq + (2 * core - 1) * jnp.asarray(offsets)
    bias = jnp.where((target >= 0) & (target < size), jnp.asarray(raise_by, f32), MASKED).astype(f32)

    pick = pl.BlockSpec((2, BLOCK, HEAD_DIM), lambda h, c: (0, 0, c[0] * heads + h))
    cut = lambda n: pl.BlockSpec((n, BLOCK, HEAD_DIM), lambda h, c: (0, 0, h))
    const = lambda *dims: pl.BlockSpec(dims, lambda h, c: (0, 0))
    derive = _derive_matrix()
    spread = _own_matrix()[0:64, 0:BLOCK].T.copy()
    outs = [((2 * BLOCK, half), bf16), ((BLOCK, half), bf16)] + [part(BLOCK, f32)] * 2 + [((4, BLOCK, half), bf16), view]
    attended, dq_mine, gp, go, gx, gy = pl.pallas_call(
        attend,
        out_shape=[jax.ShapeDtypeStruct(s, d) for s, d in outs],
        grid_spec=pltpu.PrefetchScalarGridSpec(
            num_scalar_prefetch=1,
            grid=(heads,),
            in_specs=[pick] * 2
            + [pl.BlockSpec((2 * BLOCK, HEAD_DIM), lambda h, c: (0, h)), cut(2), cut(5), cut(5)]
            + [const(192, 256), const(256, 192), const(128, 64), const(2, 640)],
            out_specs=[VMEM_SPEC] * len(outs),
        ),
        compiler_params=pltpu.CompilerParams(vmem_limit_bytes=WIDE_VMEM),
    )(core_arg, keys, values, do, ones, mine, other, _bf(derive), _bf(derive.T.copy()), _bf(spread), bias)

    take = swap(gy)
    u1, u2, far = _whole(split_view, [full(136), full(72), full(48)], core_arg, gx, take, scalars=1)
    u1, u2, attended = tie((u1, u2, attended))
    v2, v1 = hop(u2, -2), hop(u1, -1)
    out = lax.all_to_all(
        attended.reshape(2 * n_head, -1, half), ("seq", "head"), 0, 0, axis_index_groups=chip_groups, tiled=True
    )
    v1, v2, out = tie((v1, v2, out))

    u3, u6 = _whole(fold_on, [full(32), full(16)], far, v1, v2, _bf(_pass_matrix().T.copy()))
    v3, v6 = hop(u3, -3), hop(u6, -6)
    keep, back = _whole(
        fold_own, [full(BLOCK, f32), full(BLOCK)], core_arg, v1, v2, v3, v6, gp, go, _bf(_final_matrix()), scalars=1
    )
    back, out, dq_mine, dq_take = tie((back, out, dq_mine, take[4]))
    out = out.reshape(2, n_head, -1, half).transpose(2, 1, 0, 3).reshape(-1, n_head * width)
    query_gradient = jnp.concatenate(
        [jnp.where(core == 0, dq_mine, dq_take), jnp.where(core == 0, dq_take, dq_mine)], axis=1
    )
    key_gradient, value_gradient = pl.pallas_call(
        finish,
        out_shape=[jax.ShapeDtypeStruct((BLOCK, width), bf16)] * 2,
        in_specs=[VMEM_SPEC] * 2,
        compiler_params=pltpu.CompilerParams(vmem_limit_bytes=VMEM),
    )(keep, swap(back))
    return (out, query_gradient, key_gradient, value_gradient)


def solution(mesh):
    placed = (P("seq", "head"), P("seq", "head"), P("seq", "head"), P(("seq", "head"), None))
    return jax.shard_map(
        local,
        mesh=mesh,
        in_specs=placed,
        out_specs=(P(("seq", "head"), None), P("seq", "head"), P("seq", "head"), P("seq", "head")),
        check_vma=False,
    )
```

```python
import math

import jax
import jax.numpy as jnp
import numpy as np
from jax import lax
from jax.experimental import pallas as pl
from jax.experimental.pallas import tpu as pltpu
from jax.sharding import PartitionSpec as P

HEAD_DIM = 128
BLOCK = 128
BLOCKS = 128
LOG_TWO = math.log(2.0)
MASKED = -1e30
SCALE = 1.0 / math.sqrt(HEAD_DIM)
VMEM = 4 * 1024 * 1024
WIDE_VMEM = 40 * 1024 * 1024
FULL_VMEM = 56 * 1024 * 1024
HALF = 512
PER_STEP = 2

SIDE_LEVELS = [0] + [1] + [2] * 2 + [3] * 4 + [4] * 8
VIEW = {1: [1, 2, 7, 8, 13, 14], 2: [3, 4, 9, 10, 15], 3: [5, 6], 6: [11, 12]}
VIEW_BLOCKS = VIEW[1] + VIEW[2] + VIEW[3] + VIEW[6]
FAR_BLOCKS = VIEW[3] + VIEW[6]
LEVEL_ORDER = [(level, block) for level in (1, 2, 3, 4) for block in "PO"]


def _rows(level):
    return BLOCK >> level


def _starts(blocks, level_of):
    starts, row = {}, 0
    for k in blocks:
        starts[k] = row
        row += _rows(level_of(k))
    return starts, row


def _finest(k):
    return SIDE_LEVELS[k]


def _pool(matrix, row, col, rows, factor):
    for r in range(rows):
        matrix[row + r, col + r * factor : col + (r + 1) * factor] = 1.0 / factor


def _own_matrix():
    m = np.zeros((240, 256), np.float32)
    row = 0
    for level, block in LEVEL_ORDER:
        _pool(m, row, 0 if block == "P" else BLOCK, _rows(level), 1 << level)
        row += _rows(level)
    return m


def _own_rows(level, block):
    row = 0
    for entry in LEVEL_ORDER:
        if entry == (level, block):
            return row, row + _rows(level)
        row += _rows(entry[0])
    raise KeyError


def _own_sent(distance):
    return [(_finest(2 * distance - 1), "O"), (_finest(2 * distance), "P")]


def _pass_matrix():
    cols, width = _starts(FAR_BLOCKS, _finest)
    sent = [(k, 1) for k in VIEW[1][2:]] + [(k, 2) for k in VIEW[2][2:]]
    m = np.zeros((sum(_rows(_finest(k)) for k, _ in sent), width), np.float32)
    row = 0
    for k, distance in sent:
        held = k - 2 * distance
        _pool(m, row, cols[held], _rows(_finest(k)), 1 << (_finest(k) - _finest(held)))
        row += _rows(_finest(k))
    return m


def _derive_matrix():
    cols, width = _starts(VIEW_BLOCKS, _finest)
    blocks = [k for k in VIEW_BLOCKS if k < 15]
    rows, height = _starts(blocks, lambda k: SIDE_LEVELS[k + 1])
    m = np.zeros((height, width), np.float32)
    for k in blocks:
        level = SIDE_LEVELS[k + 1]
        _pool(m, rows[k], cols[k], _rows(level), 1 << (level - _finest(k)))
    return m


def _final_matrix():
    own = _own_matrix()
    m = np.zeros((256, 256), np.float32)
    row = 0
    for distance, blocks in VIEW.items():
        start = row
        for level, block in _own_sent(distance):
            first, last = _own_rows(level, block)
            m[start : start + last - first] = own[first:last]
            start += last - first
        row += sum(_rows(_finest(k)) for k in blocks)
    return m.T.copy()


def _bias_tables():
    derived = [(k, SIDE_LEVELS[k + 1]) for k in VIEW_BLOCKS if k < 15]
    direct = [(k, _finest(k)) for k in VIEW_BLOCKS]
    p = [(0, 0, 128), (-1, 1, 64)] + [(k, lv, _rows(lv)) for k, lv in direct] + [(-1 - k, lv, _rows(lv)) for k, lv in derived]
    o = [(-1, 0, 128), (0, 1, 64)] + [(-1 - k, lv, _rows(lv)) for k, lv in direct] + [(k, lv, _rows(lv)) for k, lv in derived]
    table = np.array([[(off, lv) for off, lv, n in part for _ in range(n)] for part in (p, o)], np.int32)
    return table[..., 0], table[..., 1].astype(np.float32) * LOG_TWO


def _bf(m):
    return jnp.asarray(m, jnp.bfloat16)


def _dot(a, b):
    return jnp.dot(a, b, preferred_element_type=jnp.float32)


def _pull(a, b):
    return lax.dot_general(a, b, (((0,), (0,)), ((), ())), preferred_element_type=jnp.float32)


def _outer(a, b):
    return lax.dot_general(a, b, (((1,), (1,)), ((), ())), preferred_element_type=jnp.float32)


def _wide(*parts):
    return jnp.concatenate([p.astype(jnp.float32) for p in parts], axis=0)


def _half(core):
    return pl.ds(pl.multiple_of(core * HALF, HALF), HALF)


def pack_coarse(k_ref, v_ref, out_ref):
    row = lax.broadcasted_iota(jnp.int32, (32, BLOCK), 0)
    col = lax.broadcasted_iota(jnp.int32, (32, BLOCK), 1)
    three = jnp.where(row == (col >> 3), 0.125, 0.0)
    pool = jnp.where(row - 16 == (col >> 4), 0.0625, three).astype(jnp.bfloat16)
    for part, ref in enumerate((k_ref, v_ref)):
        out_ref[part] = _dot(pool, ref[...]).astype(jnp.bfloat16)


def pack_far(core_ref, both_ref, three_ref, six_ref):
    core = core_ref[0]
    for part in range(2):
        mine, other = both_ref[core, part], both_ref[1 - core, part]
        three_ref[part, 0:16] = other[0:16]
        three_ref[part, 16:32] = mine[0:16]
        fours = [rows[16:32].astype(jnp.float32)[0:8] for rows in (other, mine)]
        six_ref[part] = jnp.concatenate(fours, axis=0).astype(jnp.bfloat16)


def pack_own(core_ref, k_ref, v_ref, own_ref, one_own_ref, two_own_ref, ones_ref):
    core = core_ref[0]
    for part, ref in enumerate((k_ref, v_ref)):
        levels = _dot(own_ref[...], jnp.concatenate([ref[core], ref[1 - core]], axis=0))
        for out, distance in ((one_own_ref, 1), (two_own_ref, 2)):
            spans = [_own_rows(level, block) for level, block in _own_sent(distance)]
            out[part] = jnp.concatenate([levels[a:b] for a, b in spans], axis=0).astype(jnp.bfloat16)
        one_own = jnp.concatenate([ref[core, :, _half(core)], ref[1 - core, :, _half(core)]], axis=0)
        ones_ref[part] = _dot(own_ref[0:128], one_own).astype(jnp.bfloat16)


def pack_on(three_ref, six_ref, one_own_ref, two_own_ref, w_ref, one_ref, two_ref):
    for part in range(2):
        on = _dot(w_ref[...], jnp.concatenate([three_ref[part], six_ref[part]], axis=0))
        one_ref[part] = _wide(one_own_ref[part], on[0:40]).astype(jnp.bfloat16)
        two_ref[part] = _wide(two_own_ref[part], on[40:64]).astype(jnp.bfloat16)


def join_view(core_ref, one_ref, two_ref, three_ref, six_ref, q_ref, mine_ref, give_ref):
    core = core_ref[0]
    for out, lanes in ((mine_ref, _half(core)), (give_ref, _half(1 - core))):
        for part in range(2):
            near = _wide(one_ref[part, :, lanes], two_ref[part, :, lanes]).astype(jnp.bfloat16)
            out[2 * part] = near[0:128]
            out[2 * part + 1, 0:80] = near[128:208]
            out[2 * part + 1, 80:112] = three_ref[part, :, lanes]
            out[2 * part + 1, 112:128] = six_ref[part, :, lanes]
        out[4] = q_ref[:, lanes]


def attend(
    core_ref, k_ref, v_ref, do_ref, ones_ref, x_ref, y_ref, derive_ref, derive_t_ref, spread_ref, bias_ref,
    o_ref, dq_ref, gp_ref, go_ref, gx_ref, gy_ref,
):
    core = core_ref[0]
    width = PER_STEP * HEAD_DIM
    lanes = pl.ds(pl.multiple_of(pl.program_id(0) * width, width), width)
    sets_p, sets_o = [], []
    for part, ref in enumerate((k_ref, v_ref)):
        x = jnp.concatenate([x_ref[2 * part], x_ref[2 * part + 1]], axis=0)
        y = jnp.concatenate([y_ref[2 * part], y_ref[2 * part + 1]], axis=0)
        x_derived = _dot(derive_ref[...], x).astype(jnp.bfloat16)
        y_derived = _dot(derive_ref[...], y).astype(jnp.bfloat16)
        sets_p.append(jnp.concatenate([ref[core], ones_ref[part, 64:128], x, y_derived], axis=0))
        sets_o.append(jnp.concatenate([ref[1 - core], ones_ref[part, 0:64], y, x_derived], axis=0))
    here = [pl.ds(pl.multiple_of(place * BLOCK, BLOCK), BLOCK) for place in (core, 1 - core)]
    items = []
    for head in range(PER_STEP):
        cols = slice(head * HEAD_DIM, (head + 1) * HEAD_DIM)
        for block, (keys, values) in enumerate((sets_p, sets_o)):
            q = (x_ref, y_ref)[block][4, :, cols]
            items.append((block, keys[:, cols], values[:, cols], q, do_ref[here[block], cols]))
    scores = [_outer(q, keys) for _, keys, _, q, _ in items]
    weight_grads = [_outer(do, values) for _, _, values, _, do in items]
    lows, score_grads = [], []
    for (block, *_), raw, weight_grad in zip(items, scores, weight_grads, strict=True):
        biased = raw * SCALE + bias_ref[block : block + 1]
        raised = jnp.exp(biased - jnp.max(biased, axis=1, keepdims=True))
        weights = raised * (1.0 / jnp.sum(raised, axis=1, keepdims=True))
        row_term = jnp.sum(weights * weight_grad, axis=1, keepdims=True)
        lows.append(weights.astype(jnp.bfloat16))
        score_grads.append((weights * ((weight_grad - row_term) * SCALE)).astype(jnp.bfloat16))
    outs, dqs, dks, dvs = [], [], [], []
    for (_, keys, values, q, do), low, score_grad in zip(items, lows, score_grads, strict=True):
        outs.append(_dot(low, values))
        dqs.append(_dot(score_grad, keys))
        dks.append(_pull(score_grad, q))
        dvs.append(_pull(low, do))

    def heads_of(results, block):
        return jnp.concatenate(results[block::2], axis=1)

    for block in range(2):
        o_ref[here[block], lanes] = heads_of(outs, block).astype(jnp.bfloat16)
    dq_ref[:, lanes] = heads_of(dqs, 0).astype(jnp.bfloat16)
    gy_ref[4, :, lanes] = heads_of(dqs, 1).astype(jnp.bfloat16)
    for part, results in enumerate((dks, dvs)):
        gp, go = heads_of(results, 0), heads_of(results, 1)
        gx = gp[192:448] + _dot(derive_t_ref[...], go[448:640].astype(jnp.bfloat16))
        gy = go[192:448] + _dot(derive_t_ref[...], gp[448:640].astype(jnp.bfloat16))
        for g, ref in ((gx, gx_ref), (gy, gy_ref)):
            ref[2 * part, :, lanes] = g[0:128].astype(jnp.bfloat16)
            ref[2 * part + 1, :, lanes] = g[128:256].astype(jnp.bfloat16)
        gp_ref[part, :, lanes] = gp[0:128] + _dot(spread_ref[...], go[128:192].astype(jnp.bfloat16))
        go_ref[part, :, lanes] = go[0:128] + _dot(spread_ref[...], gp[128:192].astype(jnp.bfloat16))


def split_view(core_ref, mine_ref, take_ref, one_ref, two_ref, far_ref):
    core = core_ref[0]
    for src, lanes in ((mine_ref, _half(core)), (take_ref, _half(1 - core))):
        for part in range(2):
            near = _wide(src[2 * part], src[2 * part + 1, 0:80])
            one_ref[part, :, lanes] = near[0:136].astype(jnp.bfloat16)
            two_ref[part, :, lanes] = near[136:208].astype(jnp.bfloat16)
            far_ref[part, :, lanes] = src[2 * part + 1, 80:128]


def fold_on(far_ref, one_ref, two_ref, w_ref, three_ref, six_ref):
    for part in range(2):
        back = _wide(one_ref[part], two_ref[part])
        on = jnp.concatenate([back[96:136], back[184:208]], axis=0).astype(jnp.bfloat16)
        far = far_ref[part].astype(jnp.float32) + _dot(w_ref[...], on)
        three_ref[part] = far[0:32].astype(jnp.bfloat16)
        six_ref[part] = far[32:48].astype(jnp.bfloat16)


def fold_own(core_ref, one_ref, two_ref, three_ref, six_ref, gp_ref, go_ref, w_ref, keep_ref, give_ref):
    lanes = _half(core_ref[0])
    for part in range(2):
        near = _wide(one_ref[part], two_ref[part]).astype(jnp.bfloat16)
        total = _dot(w_ref[...], jnp.concatenate([near, three_ref[part], six_ref[part]], axis=0))
        keep_ref[part] = total[0:BLOCK]
        keep_ref[part, :, lanes] += gp_ref[part]
        give_ref[part] = total[BLOCK:].astype(jnp.bfloat16)
        give_ref[part, :, lanes] = (give_ref[part, :, lanes].astype(jnp.float32) + go_ref[part]).astype(jnp.bfloat16)


def finish(keep_ref, take_ref, k_ref, v_ref):
    for part, ref in enumerate((k_ref, v_ref)):
        ref[...] = (keep_ref[part] + take_ref[part].astype(jnp.float32)).astype(jnp.bfloat16)


VMEM_SPEC = pl.BlockSpec(memory_space=pltpu.VMEM)
SMEM_SPEC = pl.BlockSpec(memory_space=pltpu.SMEM)


def _whole(body, outs, *args, scalars=0):
    return pl.pallas_call(
        body,
        out_shape=[jax.ShapeDtypeStruct(s, d) for s, d in outs],
        in_specs=[SMEM_SPEC] * scalars + [VMEM_SPEC] * (len(args) - scalars),
        out_specs=[VMEM_SPEC] * len(outs),
        compiler_params=pltpu.CompilerParams(vmem_limit_bytes=VMEM),
    )(*args)


def local(queries, key_states, value_states, cotangent):
    bf16, f32 = jnp.bfloat16, jnp.float32
    tie = lax.optimization_barrier
    size = lax.axis_size("seq")
    seq = lax.axis_index("seq")
    core = lax.rem(seq, 2)
    width = queries.shape[1]
    half = width // 2
    n_head = lax.axis_size("head")
    chip_cores = [[2 * i, 2 * i + 1] for i in range(size // 2)]
    chip_groups = [[g * 2 * n_head + m for m in range(2 * n_head)] for g in range(size // 2)]

    def hop(x, chips):
        pairs = [(i, i + (2 - 4 * (i % 2)) * chips) for i in range(size)]
        return lax.ppermute(x, "seq", [(i, j) for i, j in pairs if 0 <= j < size])

    def swap(x):
        return lax.ppermute(x, "seq", [(i, i ^ 1) for i in range(size)])

    def both_cores(x):
        return lax.all_gather(x, "seq", axis=0, axis_index_groups=chip_cores)

    def full(n, dtype=bf16):
        return ((2, n, width), dtype)

    view = ((5, BLOCK, half), bf16)

    def part(n, dtype=bf16):
        return ((2, n, half), dtype)

    core_arg = core.reshape(1).astype(jnp.int32)
    whole_block = pl.BlockSpec((BLOCK, width), lambda i: (0, 0))
    mine = pl.pallas_call(
        pack_coarse,
        out_shape=jax.ShapeDtypeStruct(*full(32)),
        grid=(1,),
        in_specs=[whole_block] * 2,
        out_specs=VMEM_SPEC,
        compiler_params=pltpu.CompilerParams(vmem_limit_bytes=FULL_VMEM),
    )(key_states, value_states)
    t3, t6 = _whole(pack_far, [full(32), full(16)], core_arg, both_cores(mine), scalars=1)
    t3, t6, late_keys, late_values = tie((t3, t6, key_states, value_states))
    r3, r6 = hop(t3, 3), hop(t6, 6)

    keys, values = both_cores(late_keys), both_cores(late_values)
    own1, own2, ones = _whole(
        pack_own, [full(96), full(48), part(128)], core_arg, keys, values, _bf(_own_matrix()), scalars=1
    )
    r3, r6, late_cotangent = tie((r3, r6, cotangent))

    t1, t2 = _whole(pack_on, [full(136), full(72)], r3, r6, own1, own2, _bf(_pass_matrix()))
    t1, t2, late_cotangent = tie((t1, t2, late_cotangent))
    r2, r1 = hop(t2, 2), hop(t1, 1)
    split = late_cotangent.reshape(-1, n_head, 2, half).transpose(2, 1, 0, 3).reshape(2 * n_head, -1, half)
    do = lax.all_to_all(split, ("seq", "head"), 0, 0, axis_index_groups=chip_groups, tiled=True)
    do = do.reshape(2 * BLOCK, half)
    r1, r2, do = tie((r1, r2, do))
    mine, give = _whole(join_view, [view] * 2, core_arg, r1, r2, r3, r6, queries, scalars=1)
    other = swap(give)

    offsets, raise_by = _bias_tables()
    target = seq + (2 * core - 1) * jnp.asarray(offsets)
    bias = jnp.where((target >= 0) & (target < size), jnp.asarray(raise_by, f32), MASKED).astype(f32)

    step = PER_STEP * HEAD_DIM
    steps = half // step
    pick = pl.BlockSpec((2, BLOCK, step), lambda h, c: (0, 0, c[0] * steps + h))
    cut = lambda n: pl.BlockSpec((n, BLOCK, step), lambda h, c: (0, 0, h))
    const = lambda *dims: pl.BlockSpec(dims, lambda h, c: (0, 0))
    derive = _derive_matrix()
    spread = _own_matrix()[0:64, 0:BLOCK].T.copy()
    outs = [((2 * BLOCK, half), bf16), ((BLOCK, half), bf16)] + [part(BLOCK, f32)] * 2 + [((4, BLOCK, half), bf16), view]
    attended, dq_mine, gp, go, gx, gy = pl.pallas_call(
        attend,
        out_shape=[jax.ShapeDtypeStruct(s, d) for s, d in outs],
        grid_spec=pltpu.PrefetchScalarGridSpec(
            num_scalar_prefetch=1,
            grid=(steps,),
            in_specs=[pick] * 2
            + [pl.BlockSpec((2 * BLOCK, step), lambda h, c: (0, h)), cut(2), cut(5), cut(5)]
            + [const(192, 256), const(256, 192), const(128, 64), const(2, 640)],
            out_specs=[VMEM_SPEC] * len(outs),
        ),
        compiler_params=pltpu.CompilerParams(vmem_limit_bytes=WIDE_VMEM),
    )(core_arg, keys, values, do, ones, mine, other, _bf(derive), _bf(derive.T.copy()), _bf(spread), bias)

    take = swap(gy)
    u1, u2, far = _whole(split_view, [full(136), full(72), full(48)], core_arg, gx, take, scalars=1)
    u1, u2, attended = tie((u1, u2, attended))
    v2, v1 = hop(u2, -2), hop(u1, -1)
    out = lax.all_to_all(
        attended.reshape(2 * n_head, -1, half), ("seq", "head"), 0, 0, axis_index_groups=chip_groups, tiled=True
    )
    v1, v2, out = tie((v1, v2, out))

    u3, u6 = _whole(fold_on, [full(32), full(16)], far, v1, v2, _bf(_pass_matrix().T.copy()))
    v3, v6 = hop(u3, -3), hop(u6, -6)
    keep, back = _whole(
        fold_own, [full(BLOCK, f32), full(BLOCK)], core_arg, v1, v2, v3, v6, gp, go, _bf(_final_matrix()), scalars=1
    )
    back, out, dq_mine, dq_take = tie((back, out, dq_mine, take[4]))
    out = out.reshape(2, n_head, -1, half).transpose(2, 1, 0, 3).reshape(-1, n_head * width)
    query_gradient = jnp.concatenate(
        [jnp.where(core == 0, dq_mine, dq_take), jnp.where(core == 0, dq_take, dq_mine)], axis=1
    )
    key_gradient, value_gradient = pl.pallas_call(
        finish,
        out_shape=[jax.ShapeDtypeStruct((BLOCK, width), bf16)] * 2,
        in_specs=[VMEM_SPEC] * 2,
        compiler_params=pltpu.CompilerParams(vmem_limit_bytes=VMEM),
    )(keep, swap(back))
    return (out, query_gradient, key_gradient, value_gradient)


def solution(mesh):
    placed = (P("seq", "head"), P("seq", "head"), P("seq", "head"), P(("seq", "head"), None))
    return jax.shard_map(
        local,
        mesh=mesh,
        in_specs=placed,
        out_specs=(P(("seq", "head"), None), P("seq", "head"), P("seq", "head"), P("seq", "head")),
        check_vma=False,
    )
```

```python
import math

import jax
import jax.numpy as jnp
import numpy as np
from jax import lax
from jax.experimental import pallas as pl
from jax.experimental.pallas import tpu as pltpu
from jax.sharding import PartitionSpec as P

HEAD_DIM = 128
BLOCK = 128
BLOCKS = 128
LOG_TWO = math.log(2.0)
MASKED = -1e30
SCALE = 1.0 / math.sqrt(HEAD_DIM)
VMEM = 4 * 1024 * 1024
WIDE_VMEM = 28 * 1024 * 1024
FULL_VMEM = 56 * 1024 * 1024
HALF = 512
PER_STEP = 2
SPANS = 4

SIDE_LEVELS = [0] + [1] + [2] * 2 + [3] * 4 + [4] * 8
VIEW = {1: [1, 2, 7, 8, 13, 14], 2: [3, 4, 9, 10, 15], 3: [5, 6], 6: [11, 12]}
VIEW_BLOCKS = VIEW[1] + VIEW[2] + VIEW[3] + VIEW[6]
FAR_BLOCKS = VIEW[3] + VIEW[6]
LEVEL_ORDER = [(level, block) for level in (1, 2, 3, 4) for block in "PO"]


def _rows(level):
    return BLOCK >> level


def _starts(blocks, level_of):
    starts, row = {}, 0
    for k in blocks:
        starts[k] = row
        row += _rows(level_of(k))
    return starts, row


def _finest(k):
    return SIDE_LEVELS[k]


def _pool(matrix, row, col, rows, factor):
    for r in range(rows):
        matrix[row + r, col + r * factor : col + (r + 1) * factor] = 1.0 / factor


def _own_matrix():
    m = np.zeros((240, 256), np.float32)
    row = 0
    for level, block in LEVEL_ORDER:
        _pool(m, row, 0 if block == "P" else BLOCK, _rows(level), 1 << level)
        row += _rows(level)
    return m


def _own_rows(level, block):
    row = 0
    for entry in LEVEL_ORDER:
        if entry == (level, block):
            return row, row + _rows(level)
        row += _rows(entry[0])
    raise KeyError


def _own_sent(distance):
    return [(_finest(2 * distance - 1), "O"), (_finest(2 * distance), "P")]


def _pass_matrix():
    cols, width = _starts(FAR_BLOCKS, _finest)
    sent = [(k, 1) for k in VIEW[1][2:]] + [(k, 2) for k in VIEW[2][2:]]
    m = np.zeros((sum(_rows(_finest(k)) for k, _ in sent), width), np.float32)
    row = 0
    for k, distance in sent:
        held = k - 2 * distance
        _pool(m, row, cols[held], _rows(_finest(k)), 1 << (_finest(k) - _finest(held)))
        row += _rows(_finest(k))
    return m


def _derive_matrix():
    cols, width = _starts(VIEW_BLOCKS, _finest)
    blocks = [k for k in VIEW_BLOCKS if k < 15]
    rows, height = _starts(blocks, lambda k: SIDE_LEVELS[k + 1])
    m = np.zeros((height, width), np.float32)
    for k in blocks:
        level = SIDE_LEVELS[k + 1]
        _pool(m, rows[k], cols[k], _rows(level), 1 << (level - _finest(k)))
    return m


def _final_matrix():
    own = _own_matrix()
    m = np.zeros((256, 256), np.float32)
    row = 0
    for distance, blocks in VIEW.items():
        start = row
        for level, block in _own_sent(distance):
            first, last = _own_rows(level, block)
            m[start : start + last - first] = own[first:last]
            start += last - first
        row += sum(_rows(_finest(k)) for k in blocks)
    return m.T.copy()


def _bias_tables():
    derived = [(k, SIDE_LEVELS[k + 1]) for k in VIEW_BLOCKS if k < 15]
    direct = [(k, _finest(k)) for k in VIEW_BLOCKS]
    p = [(0, 0, 128), (-1, 1, 64)] + [(k, lv, _rows(lv)) for k, lv in direct] + [(-1 - k, lv, _rows(lv)) for k, lv in derived]
    o = [(-1, 0, 128), (0, 1, 64)] + [(-1 - k, lv, _rows(lv)) for k, lv in direct] + [(k, lv, _rows(lv)) for k, lv in derived]
    table = np.array([[(off, lv) for off, lv, n in part for _ in range(n)] for part in (p, o)], np.int32)
    return table[..., 0], table[..., 1].astype(np.float32) * LOG_TWO


def _bf(m):
    return jnp.asarray(m, jnp.bfloat16)


def _dot(a, b):
    return jnp.dot(a, b, preferred_element_type=jnp.float32)


def _pull(a, b):
    return lax.dot_general(a, b, (((0,), (0,)), ((), ())), preferred_element_type=jnp.float32)


def _outer(a, b):
    return lax.dot_general(a, b, (((1,), (1,)), ((), ())), preferred_element_type=jnp.float32)


def _wide(*parts):
    return jnp.concatenate([p.astype(jnp.float32) for p in parts], axis=0)


def _half(core):
    return pl.ds(pl.multiple_of(core * HALF, HALF), HALF)


def pack_coarse(k_ref, v_ref, out_ref):
    row = lax.broadcasted_iota(jnp.int32, (32, BLOCK), 0)
    col = lax.broadcasted_iota(jnp.int32, (32, BLOCK), 1)
    three = jnp.where(row == (col >> 3), 0.125, 0.0)
    pool = jnp.where(row - 16 == (col >> 4), 0.0625, three).astype(jnp.bfloat16)
    for part, ref in enumerate((k_ref, v_ref)):
        out_ref[part] = _dot(pool, ref[...]).astype(jnp.bfloat16)


def pack_far(core_ref, both_ref, three_ref, six_ref):
    core = core_ref[0]
    for part in range(2):
        mine, other = both_ref[core, part], both_ref[1 - core, part]
        three_ref[part, 0:16] = other[0:16]
        three_ref[part, 16:32] = mine[0:16]
        fours = [rows[16:32].astype(jnp.float32)[0:8] for rows in (other, mine)]
        six_ref[part] = jnp.concatenate(fours, axis=0).astype(jnp.bfloat16)


def pack_own(core_ref, k_ref, v_ref, own_ref, one_own_ref, two_own_ref, ones_ref):
    core = core_ref[0]
    for part, ref in enumerate((k_ref, v_ref)):
        levels = _dot(own_ref[...], jnp.concatenate([ref[core], ref[1 - core]], axis=0))
        for out, distance in ((one_own_ref, 1), (two_own_ref, 2)):
            spans = [_own_rows(level, block) for level, block in _own_sent(distance)]
            out[part] = jnp.concatenate([levels[a:b] for a, b in spans], axis=0).astype(jnp.bfloat16)
        one_own = jnp.concatenate([ref[core, :, _half(core)], ref[1 - core, :, _half(core)]], axis=0)
        ones_ref[part] = _dot(own_ref[0:128], one_own).astype(jnp.bfloat16)


def pack_on(three_ref, six_ref, one_own_ref, two_own_ref, w_ref, one_ref, two_ref):
    for part in range(2):
        on = _dot(w_ref[...], jnp.concatenate([three_ref[part], six_ref[part]], axis=0))
        one_ref[part] = _wide(one_own_ref[part], on[0:40]).astype(jnp.bfloat16)
        two_ref[part] = _wide(two_own_ref[part], on[40:64]).astype(jnp.bfloat16)


def join_view(core_ref, one_ref, two_ref, three_ref, six_ref, q_ref, mine_ref, give_ref):
    core = core_ref[0]
    for out, lanes in ((mine_ref, _half(core)), (give_ref, _half(1 - core))):
        for part in range(2):
            near = _wide(one_ref[part, :, lanes], two_ref[part, :, lanes]).astype(jnp.bfloat16)
            out[2 * part] = near[0:128]
            out[2 * part + 1, 0:80] = near[128:208]
            out[2 * part + 1, 80:112] = three_ref[part, :, lanes]
            out[2 * part + 1, 112:128] = six_ref[part, :, lanes]
        out[4] = q_ref[:, lanes]


def attend(
    core_ref, k_ref, v_ref, do_ref, ones_ref, x_ref, y_ref, derive_ref, derive_t_ref, spread_ref, bias_ref,
    o_ref, dq_ref, gp_ref, go_ref, gx_ref, gy_ref,
):
    core = core_ref[0]
    width = PER_STEP * HEAD_DIM
    lanes = pl.ds(pl.multiple_of(pl.program_id(0) * width, width), width)
    sets_p, sets_o = [], []
    for part, ref in enumerate((k_ref, v_ref)):
        x = jnp.concatenate([x_ref[2 * part], x_ref[2 * part + 1]], axis=0)
        y = jnp.concatenate([y_ref[2 * part], y_ref[2 * part + 1]], axis=0)
        x_derived = _dot(derive_ref[...], x).astype(jnp.bfloat16)
        y_derived = _dot(derive_ref[...], y).astype(jnp.bfloat16)
        sets_p.append(jnp.concatenate([ref[core], ones_ref[part, 64:128], x, y_derived], axis=0))
        sets_o.append(jnp.concatenate([ref[1 - core], ones_ref[part, 0:64], y, x_derived], axis=0))
    span = BLOCK // SPANS
    here = [
        [pl.ds(pl.multiple_of((2 * i + place) * span, span), span) for i in range(SPANS)] for place in (core, 1 - core)
    ]
    items = []
    for head in range(PER_STEP):
        cols = slice(head * HEAD_DIM, (head + 1) * HEAD_DIM)
        for block, (keys, values) in enumerate((sets_p, sets_o)):
            q = (x_ref, y_ref)[block][4, :, cols]
            do = jnp.concatenate([do_ref[rows, cols] for rows in here[block]], axis=0)
            items.append((block, keys[:, cols], values[:, cols], q, do))
    scores = [_outer(q, keys) for _, keys, _, q, _ in items]
    weight_grads = [_outer(do, values) for _, _, values, _, do in items]
    lows, score_grads = [], []
    for (block, *_), raw, weight_grad in zip(items, scores, weight_grads, strict=True):
        biased = raw * SCALE + bias_ref[block : block + 1]
        raised = jnp.exp(biased - jnp.max(biased, axis=1, keepdims=True))
        weights = raised * (1.0 / jnp.sum(raised, axis=1, keepdims=True))
        row_term = jnp.sum(weights * weight_grad, axis=1, keepdims=True)
        lows.append(weights.astype(jnp.bfloat16))
        score_grads.append((weights * ((weight_grad - row_term) * SCALE)).astype(jnp.bfloat16))
    outs, dqs, dks, dvs = [], [], [], []
    for (_, keys, values, q, do), low, score_grad in zip(items, lows, score_grads, strict=True):
        outs.append(_dot(low, values))
        dqs.append(_dot(score_grad, keys))
        dks.append(_pull(score_grad, q))
        dvs.append(_pull(low, do))

    def heads_of(results, block):
        return jnp.concatenate(results[block::2], axis=1)

    for block in range(2):
        out = heads_of(outs, block).astype(jnp.bfloat16)
        for i, rows in enumerate(here[block]):
            o_ref[rows, lanes] = out[i * span : (i + 1) * span]
    dq_ref[:, lanes] = heads_of(dqs, 0).astype(jnp.bfloat16)
    gy_ref[4, :, lanes] = heads_of(dqs, 1).astype(jnp.bfloat16)
    for part, results in enumerate((dks, dvs)):
        gp, go = heads_of(results, 0), heads_of(results, 1)
        gx = gp[192:448] + _dot(derive_t_ref[...], go[448:640].astype(jnp.bfloat16))
        gy = go[192:448] + _dot(derive_t_ref[...], gp[448:640].astype(jnp.bfloat16))
        for g, ref in ((gx, gx_ref), (gy, gy_ref)):
            ref[2 * part, :, lanes] = g[0:128].astype(jnp.bfloat16)
            ref[2 * part + 1, :, lanes] = g[128:256].astype(jnp.bfloat16)
        gp_ref[part, :, lanes] = gp[0:128] + _dot(spread_ref[...], go[128:192].astype(jnp.bfloat16))
        go_ref[part, :, lanes] = go[0:128] + _dot(spread_ref[...], gp[128:192].astype(jnp.bfloat16))


def split_view(core_ref, mine_ref, take_ref, one_ref, two_ref, far_ref):
    core = core_ref[0]
    for src, lanes in ((mine_ref, _half(core)), (take_ref, _half(1 - core))):
        for part in range(2):
            near = _wide(src[2 * part], src[2 * part + 1, 0:80])
            one_ref[part, :, lanes] = near[0:136].astype(jnp.bfloat16)
            two_ref[part, :, lanes] = near[136:208].astype(jnp.bfloat16)
            far_ref[part, :, lanes] = src[2 * part + 1, 80:128]


def fold_on(far_ref, one_ref, two_ref, w_ref, three_ref, six_ref):
    for part in range(2):
        back = _wide(one_ref[part], two_ref[part])
        on = jnp.concatenate([back[96:136], back[184:208]], axis=0).astype(jnp.bfloat16)
        far = far_ref[part].astype(jnp.float32) + _dot(w_ref[...], on)
        three_ref[part] = far[0:32].astype(jnp.bfloat16)
        six_ref[part] = far[32:48].astype(jnp.bfloat16)


def fold_own(core_ref, one_ref, two_ref, three_ref, six_ref, gp_ref, go_ref, w_ref, keep_ref, give_ref):
    lanes = _half(core_ref[0])
    for part in range(2):
        near = _wide(one_ref[part], two_ref[part]).astype(jnp.bfloat16)
        total = _dot(w_ref[...], jnp.concatenate([near, three_ref[part], six_ref[part]], axis=0))
        keep_ref[part] = total[0:BLOCK]
        keep_ref[part, :, lanes] += gp_ref[part]
        give_ref[part] = total[BLOCK:].astype(jnp.bfloat16)
        give_ref[part, :, lanes] = (give_ref[part, :, lanes].astype(jnp.float32) + go_ref[part]).astype(jnp.bfloat16)


def finish(keep_ref, take_ref, k_ref, v_ref):
    for part, ref in enumerate((k_ref, v_ref)):
        ref[...] = (keep_ref[part] + take_ref[part].astype(jnp.float32)).astype(jnp.bfloat16)


VMEM_SPEC = pl.BlockSpec(memory_space=pltpu.VMEM)
SMEM_SPEC = pl.BlockSpec(memory_space=pltpu.SMEM)


def _whole(body, outs, *args, scalars=0):
    return pl.pallas_call(
        body,
        out_shape=[jax.ShapeDtypeStruct(s, d) for s, d in outs],
        in_specs=[SMEM_SPEC] * scalars + [VMEM_SPEC] * (len(args) - scalars),
        out_specs=[VMEM_SPEC] * len(outs),
        compiler_params=pltpu.CompilerParams(vmem_limit_bytes=VMEM),
    )(*args)


def local(queries, key_states, value_states, cotangent):
    bf16, f32 = jnp.bfloat16, jnp.float32
    tie = lax.optimization_barrier
    size = lax.axis_size("seq")
    seq = lax.axis_index("seq")
    core = lax.rem(seq, 2)
    width = queries.shape[1]
    half = width // 2
    n_head = lax.axis_size("head")
    chip_cores = [[2 * i, 2 * i + 1] for i in range(size // 2)]
    chip_groups = [
        [(2 * g + c) * n_head + h for h in range(n_head) for c in range(2)] for g in range(size // 2)
    ]

    def hop(x, chips):
        pairs = [(i, i + (2 - 4 * (i % 2)) * chips) for i in range(size)]
        return lax.ppermute(x, "seq", [(i, j) for i, j in pairs if 0 <= j < size])

    def swap(x):
        return lax.ppermute(x, "seq", [(i, i ^ 1) for i in range(size)])

    def both_cores(x):
        return lax.all_gather(x, "seq", axis=0, axis_index_groups=chip_cores)

    def full(n, dtype=bf16):
        return ((2, n, width), dtype)

    view = ((5, BLOCK, half), bf16)

    def part(n, dtype=bf16):
        return ((2, n, half), dtype)

    core_arg = core.reshape(1).astype(jnp.int32)
    whole_block = pl.BlockSpec((BLOCK, width), lambda i: (0, 0))
    mine = pl.pallas_call(
        pack_coarse,
        out_shape=jax.ShapeDtypeStruct(*full(32)),
        grid=(1,),
        in_specs=[whole_block] * 2,
        out_specs=VMEM_SPEC,
        compiler_params=pltpu.CompilerParams(vmem_limit_bytes=FULL_VMEM),
    )(key_states, value_states)
    t3, t6 = _whole(pack_far, [full(32), full(16)], core_arg, both_cores(mine), scalars=1)
    t3, t6, late_keys, late_values = tie((t3, t6, key_states, value_states))
    r3, r6 = hop(t3, 3), hop(t6, 6)

    keys, values = both_cores(late_keys), both_cores(late_values)
    own1, own2, ones = _whole(
        pack_own, [full(96), full(48), part(128)], core_arg, keys, values, _bf(_own_matrix()), scalars=1
    )
    r3, r6, late_cotangent = tie((r3, r6, cotangent))

    t1, t2 = _whole(pack_on, [full(136), full(72)], r3, r6, own1, own2, _bf(_pass_matrix()))
    t1, t2, late_cotangent = tie((t1, t2, late_cotangent))
    r2, r1 = hop(t2, 2), hop(t1, 1)
    split = late_cotangent.reshape(-1, 2 * n_head, half).transpose(1, 0, 2)
    do = lax.all_to_all(split, ("seq", "head"), 0, 0, axis_index_groups=chip_groups, tiled=True)
    do = do.reshape(2 * BLOCK, half)
    r1, r2, do = tie((r1, r2, do))
    mine, give = _whole(join_view, [view] * 2, core_arg, r1, r2, r3, r6, queries, scalars=1)
    other = swap(give)

    offsets, raise_by = _bias_tables()
    target = seq + (2 * core - 1) * jnp.asarray(offsets)
    bias = jnp.where((target >= 0) & (target < size), jnp.asarray(raise_by, f32), MASKED).astype(f32)

    step = PER_STEP * HEAD_DIM
    steps = half // step
    pick = pl.BlockSpec((2, BLOCK, step), lambda h, c: (0, 0, c[0] * steps + h))
    cut = lambda n: pl.BlockSpec((n, BLOCK, step), lambda h, c: (0, 0, h))
    const = lambda *dims: pl.BlockSpec(dims, lambda h, c: (0, 0))
    derive = _derive_matrix()
    spread = _own_matrix()[0:64, 0:BLOCK].T.copy()
    outs = [((2 * BLOCK, half), bf16), ((BLOCK, half), bf16)] + [part(BLOCK, f32)] * 2 + [((4, BLOCK, half), bf16), view]
    attended, dq_mine, gp, go, gx, gy = pl.pallas_call(
        attend,
        out_shape=[jax.ShapeDtypeStruct(s, d) for s, d in outs],
        grid_spec=pltpu.PrefetchScalarGridSpec(
            num_scalar_prefetch=1,
            grid=(steps,),
            in_specs=[pick] * 2
            + [pl.BlockSpec((2 * BLOCK, step), lambda h, c: (0, h)), cut(2), cut(5), cut(5)]
            + [const(192, 256), const(256, 192), const(128, 64), const(2, 640)],
            out_specs=[VMEM_SPEC] * len(outs),
        ),
        compiler_params=pltpu.CompilerParams(vmem_limit_bytes=WIDE_VMEM),
    )(core_arg, keys, values, do, ones, mine, other, _bf(derive), _bf(derive.T.copy()), _bf(spread), bias)

    take = swap(gy)
    u1, u2, far = _whole(split_view, [full(136), full(72), full(48)], core_arg, gx, take, scalars=1)
    u1, u2, attended = tie((u1, u2, attended))
    v2, v1 = hop(u2, -2), hop(u1, -1)
    out = lax.all_to_all(
        attended.reshape(2 * n_head, -1, half), ("seq", "head"), 0, 0, axis_index_groups=chip_groups, tiled=True
    )
    v1, v2, out = tie((v1, v2, out))

    u3, u6 = _whole(fold_on, [full(32), full(16)], far, v1, v2, _bf(_pass_matrix().T.copy()))
    v3, v6 = hop(u3, -3), hop(u6, -6)
    keep, back = _whole(
        fold_own, [full(BLOCK, f32), full(BLOCK)], core_arg, v1, v2, v3, v6, gp, go, _bf(_final_matrix()), scalars=1
    )
    back, out, dq_mine, dq_take = tie((back, out, dq_mine, take[4]))
    out = out.transpose(1, 0, 2).reshape(-1, n_head * width)
    query_gradient = jnp.concatenate(
        [jnp.where(core == 0, dq_mine, dq_take), jnp.where(core == 0, dq_take, dq_mine)], axis=1
    )
    key_gradient, value_gradient = pl.pallas_call(
        finish,
        out_shape=[jax.ShapeDtypeStruct((BLOCK, width), bf16)] * 2,
        in_specs=[VMEM_SPEC] * 2,
        compiler_params=pltpu.CompilerParams(vmem_limit_bytes=VMEM),
    )(keep, swap(back))
    return (out, query_gradient, key_gradient, value_gradient)


def solution(mesh):
    placed = (P("seq", "head"), P("seq", "head"), P("seq", "head"), P(("seq", "head"), None))
    return jax.shard_map(
        local,
        mesh=mesh,
        in_specs=placed,
        out_specs=(P(("seq", "head"), None), P("seq", "head"), P("seq", "head"), P("seq", "head")),
        check_vma=False,
    )
```

```python
import math

import jax
import jax.numpy as jnp
import numpy as np
from jax import lax
from jax.experimental import pallas as pl
from jax.experimental.pallas import tpu as pltpu
from jax.sharding import PartitionSpec as P

HEAD_DIM = 128
BLOCK = 128
BLOCKS = 128
LOG_TWO = math.log(2.0)
MASKED = -1e30
SCALE = 1.0 / math.sqrt(HEAD_DIM)
VMEM = 4 * 1024 * 1024
WIDE_VMEM = 28 * 1024 * 1024
FULL_VMEM = 56 * 1024 * 1024
HALF = 512
PER_STEP = 2
SPANS = 4

SIDE_LEVELS = [0] + [1] + [2] * 2 + [3] * 4 + [4] * 8
VIEW = {1: [1, 2, 7, 8, 13, 14], 2: [3, 4, 9, 10, 15], 3: [5, 6], 6: [11, 12]}
VIEW_BLOCKS = VIEW[1] + VIEW[2] + VIEW[3] + VIEW[6]
FAR_BLOCKS = VIEW[3] + VIEW[6]
LEVEL_ORDER = [(level, block) for level in (1, 2, 3, 4) for block in "PO"]


def _rows(level):
    return BLOCK >> level


def _starts(blocks, level_of):
    starts, row = {}, 0
    for k in blocks:
        starts[k] = row
        row += _rows(level_of(k))
    return starts, row


def _finest(k):
    return SIDE_LEVELS[k]


def _pool(matrix, row, col, rows, factor):
    for r in range(rows):
        matrix[row + r, col + r * factor : col + (r + 1) * factor] = 1.0 / factor


def _own_matrix():
    m = np.zeros((240, 256), np.float32)
    row = 0
    for level, block in LEVEL_ORDER:
        _pool(m, row, 0 if block == "P" else BLOCK, _rows(level), 1 << level)
        row += _rows(level)
    return m


def _own_rows(level, block):
    row = 0
    for entry in LEVEL_ORDER:
        if entry == (level, block):
            return row, row + _rows(level)
        row += _rows(entry[0])
    raise KeyError


def _own_sent(distance):
    return [(_finest(2 * distance - 1), "O"), (_finest(2 * distance), "P")]


def _pass_matrix():
    cols, width = _starts(FAR_BLOCKS, _finest)
    sent = [(k, 1) for k in VIEW[1][2:]] + [(k, 2) for k in VIEW[2][2:]]
    m = np.zeros((sum(_rows(_finest(k)) for k, _ in sent), width), np.float32)
    row = 0
    for k, distance in sent:
        held = k - 2 * distance
        _pool(m, row, cols[held], _rows(_finest(k)), 1 << (_finest(k) - _finest(held)))
        row += _rows(_finest(k))
    return m


def _derive_matrix():
    cols, width = _starts(VIEW_BLOCKS, _finest)
    blocks = [k for k in VIEW_BLOCKS if k < 15]
    rows, height = _starts(blocks, lambda k: SIDE_LEVELS[k + 1])
    m = np.zeros((height, width), np.float32)
    for k in blocks:
        level = SIDE_LEVELS[k + 1]
        _pool(m, rows[k], cols[k], _rows(level), 1 << (level - _finest(k)))
    return m


def _final_matrix():
    own = _own_matrix()
    m = np.zeros((256, 256), np.float32)
    row = 0
    for distance, blocks in VIEW.items():
        start = row
        for level, block in _own_sent(distance):
            first, last = _own_rows(level, block)
            m[start : start + last - first] = own[first:last]
            start += last - first
        row += sum(_rows(_finest(k)) for k in blocks)
    return m.T.copy()


def _bias_tables():
    derived = [(k, SIDE_LEVELS[k + 1]) for k in VIEW_BLOCKS if k < 15]
    direct = [(k, _finest(k)) for k in VIEW_BLOCKS]
    p = [(0, 0, 128), (-1, 1, 64)] + [(k, lv, _rows(lv)) for k, lv in direct] + [(-1 - k, lv, _rows(lv)) for k, lv in derived]
    o = [(-1, 0, 128), (0, 1, 64)] + [(-1 - k, lv, _rows(lv)) for k, lv in direct] + [(k, lv, _rows(lv)) for k, lv in derived]
    table = np.array([[(off, lv) for off, lv, n in part for _ in range(n)] for part in (p, o)], np.int32)
    return table[..., 0], table[..., 1].astype(np.float32) * LOG_TWO


def _bf(m):
    return jnp.asarray(m, jnp.bfloat16)


def _dot(a, b):
    return jnp.dot(a, b, preferred_element_type=jnp.float32)


def _pull(a, b):
    return lax.dot_general(a, b, (((0,), (0,)), ((), ())), preferred_element_type=jnp.float32)


def _outer(a, b):
    return lax.dot_general(a, b, (((1,), (1,)), ((), ())), preferred_element_type=jnp.float32)


def _wide(*parts):
    return jnp.concatenate([p.astype(jnp.float32) for p in parts], axis=0)


def _half(core):
    return pl.ds(pl.multiple_of(core * HALF, HALF), HALF)


def pack_coarse(k_ref, v_ref, out_ref):
    row = lax.broadcasted_iota(jnp.int32, (32, BLOCK), 0)
    col = lax.broadcasted_iota(jnp.int32, (32, BLOCK), 1)
    three = jnp.where(row == (col >> 3), 0.125, 0.0)
    pool = jnp.where(row - 16 == (col >> 4), 0.0625, three).astype(jnp.bfloat16)
    for part, ref in enumerate((k_ref, v_ref)):
        out_ref[part, :, _half(pl.program_id(0))] = _dot(pool, ref[...]).astype(jnp.bfloat16)


def pack_far(core_ref, both_ref, three_ref, six_ref):
    core = core_ref[0]
    for part in range(2):
        mine, other = both_ref[core, part], both_ref[1 - core, part]
        three_ref[part, 0:16] = other[0:16]
        three_ref[part, 16:32] = mine[0:16]
        fours = [rows[16:32].astype(jnp.float32)[0:8] for rows in (other, mine)]
        six_ref[part] = jnp.concatenate(fours, axis=0).astype(jnp.bfloat16)


def pack_own(core_ref, k_ref, v_ref, own_ref, one_own_ref, two_own_ref, ones_ref):
    core = core_ref[0]
    for part, ref in enumerate((k_ref, v_ref)):
        levels = _dot(own_ref[...], jnp.concatenate([ref[core], ref[1 - core]], axis=0))
        for out, distance in ((one_own_ref, 1), (two_own_ref, 2)):
            spans = [_own_rows(level, block) for level, block in _own_sent(distance)]
            out[part] = jnp.concatenate([levels[a:b] for a, b in spans], axis=0).astype(jnp.bfloat16)
        one_own = jnp.concatenate([ref[core, :, _half(core)], ref[1 - core, :, _half(core)]], axis=0)
        ones_ref[part] = _dot(own_ref[0:128], one_own).astype(jnp.bfloat16)


def pack_on(three_ref, six_ref, one_own_ref, two_own_ref, w_ref, one_ref, two_ref):
    for part in range(2):
        on = _dot(w_ref[...], jnp.concatenate([three_ref[part], six_ref[part]], axis=0))
        one_ref[part] = _wide(one_own_ref[part], on[0:40]).astype(jnp.bfloat16)
        two_ref[part] = _wide(two_own_ref[part], on[40:64]).astype(jnp.bfloat16)


def join_view(core_ref, one_ref, two_ref, three_ref, six_ref, q_ref, mine_ref, give_ref):
    core = core_ref[0]
    for out, lanes in ((mine_ref, _half(core)), (give_ref, _half(1 - core))):
        for part in range(2):
            near = _wide(one_ref[part, :, lanes], two_ref[part, :, lanes]).astype(jnp.bfloat16)
            out[2 * part] = near[0:128]
            out[2 * part + 1, 0:80] = near[128:208]
            out[2 * part + 1, 80:112] = three_ref[part, :, lanes]
            out[2 * part + 1, 112:128] = six_ref[part, :, lanes]
        out[4] = q_ref[:, lanes]


def attend(
    core_ref, k_ref, v_ref, do_ref, ones_ref, x_ref, y_ref, derive_ref, derive_t_ref, spread_ref, bias_ref,
    o_ref, dq_ref, gp_ref, go_ref, gx_ref, gy_ref,
):
    core = core_ref[0]
    width = PER_STEP * HEAD_DIM
    lanes = pl.ds(pl.multiple_of(pl.program_id(0) * width, width), width)
    sets_p, sets_o = [], []
    for part, ref in enumerate((k_ref, v_ref)):
        x = jnp.concatenate([x_ref[2 * part], x_ref[2 * part + 1]], axis=0)
        y = jnp.concatenate([y_ref[2 * part], y_ref[2 * part + 1]], axis=0)
        x_derived = _dot(derive_ref[...], x).astype(jnp.bfloat16)
        y_derived = _dot(derive_ref[...], y).astype(jnp.bfloat16)
        sets_p.append(jnp.concatenate([ref[core], ones_ref[part, 64:128], x, y_derived], axis=0))
        sets_o.append(jnp.concatenate([ref[1 - core], ones_ref[part, 0:64], y, x_derived], axis=0))
    span = BLOCK // SPANS
    here = [
        [pl.ds(pl.multiple_of((2 * i + place) * span, span), span) for i in range(SPANS)] for place in (core, 1 - core)
    ]
    items = []
    for head in range(PER_STEP):
        cols = slice(head * HEAD_DIM, (head + 1) * HEAD_DIM)
        for block, (keys, values) in enumerate((sets_p, sets_o)):
            q = (x_ref, y_ref)[block][4, :, cols]
            do = jnp.concatenate([do_ref[rows, cols] for rows in here[block]], axis=0)
            items.append((block, keys[:, cols], values[:, cols], q, do))
    scores = [_outer(q, keys) for _, keys, _, q, _ in items]
    weight_grads = [_outer(do, values) for _, _, values, _, do in items]
    lows, score_grads = [], []
    for (block, *_), raw, weight_grad in zip(items, scores, weight_grads, strict=True):
        biased = raw * SCALE + bias_ref[block : block + 1]
        raised = jnp.exp(biased - jnp.max(biased, axis=1, keepdims=True))
        weights = raised * (1.0 / jnp.sum(raised, axis=1, keepdims=True))
        row_term = jnp.sum(weights * weight_grad, axis=1, keepdims=True)
        lows.append(weights.astype(jnp.bfloat16))
        score_grads.append((weights * ((weight_grad - row_term) * SCALE)).astype(jnp.bfloat16))
    outs, dqs, dks, dvs = [], [], [], []
    for (_, keys, values, q, do), low, score_grad in zip(items, lows, score_grads, strict=True):
        outs.append(_dot(low, values))
        dqs.append(_dot(score_grad, keys))
        dks.append(_pull(score_grad, q))
        dvs.append(_pull(low, do))

    def heads_of(results, block):
        return jnp.concatenate(results[block::2], axis=1)

    for block in range(2):
        out = heads_of(outs, block).astype(jnp.bfloat16)
        for i, rows in enumerate(here[block]):
            o_ref[rows, lanes] = out[i * span : (i + 1) * span]
    dq_ref[:, lanes] = heads_of(dqs, 0).astype(jnp.bfloat16)
    gy_ref[4, :, lanes] = heads_of(dqs, 1).astype(jnp.bfloat16)
    for part, results in enumerate((dks, dvs)):
        gp, go = heads_of(results, 0), heads_of(results, 1)
        gx = gp[192:448] + _dot(derive_t_ref[...], go[448:640].astype(jnp.bfloat16))
        gy = go[192:448] + _dot(derive_t_ref[...], gp[448:640].astype(jnp.bfloat16))
        for g, ref in ((gx, gx_ref), (gy, gy_ref)):
            ref[2 * part, :, lanes] = g[0:128].astype(jnp.bfloat16)
            ref[2 * part + 1, :, lanes] = g[128:256].astype(jnp.bfloat16)
        gp_ref[part, :, lanes] = gp[0:128] + _dot(spread_ref[...], go[128:192].astype(jnp.bfloat16))
        go_ref[part, :, lanes] = go[0:128] + _dot(spread_ref[...], gp[128:192].astype(jnp.bfloat16))


def split_view(core_ref, mine_ref, take_ref, one_ref, two_ref, far_ref):
    core = core_ref[0]
    for src, lanes in ((mine_ref, _half(core)), (take_ref, _half(1 - core))):
        for part in range(2):
            near = _wide(src[2 * part], src[2 * part + 1, 0:80])
            one_ref[part, :, lanes] = near[0:136].astype(jnp.bfloat16)
            two_ref[part, :, lanes] = near[136:208].astype(jnp.bfloat16)
            far_ref[part, :, lanes] = src[2 * part + 1, 80:128]


def fold_on(far_ref, one_ref, two_ref, w_ref, three_ref, six_ref):
    for part in range(2):
        back = _wide(one_ref[part], two_ref[part])
        on = jnp.concatenate([back[96:136], back[184:208]], axis=0).astype(jnp.bfloat16)
        far = far_ref[part].astype(jnp.float32) + _dot(w_ref[...], on)
        three_ref[part] = far[0:32].astype(jnp.bfloat16)
        six_ref[part] = far[32:48].astype(jnp.bfloat16)


def fold_own(core_ref, one_ref, two_ref, three_ref, six_ref, gp_ref, go_ref, w_ref, keep_ref, give_ref):
    lanes = _half(core_ref[0])
    for part in range(2):
        near = _wide(one_ref[part], two_ref[part]).astype(jnp.bfloat16)
        total = _dot(w_ref[...], jnp.concatenate([near, three_ref[part], six_ref[part]], axis=0))
        keep_ref[part] = total[0:BLOCK]
        keep_ref[part, :, lanes] += gp_ref[part]
        give_ref[part] = total[BLOCK:].astype(jnp.bfloat16)
        give_ref[part, :, lanes] = (give_ref[part, :, lanes].astype(jnp.float32) + go_ref[part]).astype(jnp.bfloat16)


def finish(keep_ref, take_ref, k_ref, v_ref):
    for part, ref in enumerate((k_ref, v_ref)):
        ref[...] = (keep_ref[part] + take_ref[part].astype(jnp.float32)).astype(jnp.bfloat16)


VMEM_SPEC = pl.BlockSpec(memory_space=pltpu.VMEM)
SMEM_SPEC = pl.BlockSpec(memory_space=pltpu.SMEM)


def _whole(body, outs, *args, scalars=0):
    return pl.pallas_call(
        body,
        out_shape=[jax.ShapeDtypeStruct(s, d) for s, d in outs],
        in_specs=[SMEM_SPEC] * scalars + [VMEM_SPEC] * (len(args) - scalars),
        out_specs=[VMEM_SPEC] * len(outs),
        compiler_params=pltpu.CompilerParams(vmem_limit_bytes=VMEM),
    )(*args)


def local(queries, key_states, value_states, cotangent):
    bf16, f32 = jnp.bfloat16, jnp.float32
    tie = lax.optimization_barrier
    size = lax.axis_size("seq")
    seq = lax.axis_index("seq")
    core = lax.rem(seq, 2)
    width = queries.shape[1]
    half = width // 2
    n_head = lax.axis_size("head")
    chip_cores = [[2 * i, 2 * i + 1] for i in range(size // 2)]
    chip_groups = [
        [(2 * g + c) * n_head + h for h in range(n_head) for c in range(2)] for g in range(size // 2)
    ]

    def hop(x, chips):
        pairs = [(i, i + (2 - 4 * (i % 2)) * chips) for i in range(size)]
        return lax.ppermute(x, "seq", [(i, j) for i, j in pairs if 0 <= j < size])

    def swap(x):
        return lax.ppermute(x, "seq", [(i, i ^ 1) for i in range(size)])

    def both_cores(x):
        return lax.all_gather(x, "seq", axis=0, axis_index_groups=chip_cores)

    def full(n, dtype=bf16):
        return ((2, n, width), dtype)

    view = ((5, BLOCK, half), bf16)

    def part(n, dtype=bf16):
        return ((2, n, half), dtype)

    core_arg = core.reshape(1).astype(jnp.int32)
    half_block = pl.BlockSpec((BLOCK, half), lambda i: (0, i))
    mine = pl.pallas_call(
        pack_coarse,
        out_shape=jax.ShapeDtypeStruct(*full(32)),
        grid=(2,),
        in_specs=[half_block] * 2,
        out_specs=VMEM_SPEC,
        compiler_params=pltpu.CompilerParams(vmem_limit_bytes=FULL_VMEM),
    )(key_states, value_states)
    t3, t6 = _whole(pack_far, [full(32), full(16)], core_arg, both_cores(mine), scalars=1)
    t3, t6, late_keys, late_values = tie((t3, t6, key_states, value_states))
    r3, r6 = hop(t3, 3), hop(t6, 6)

    keys, values = both_cores(late_keys), both_cores(late_values)
    own1, own2, ones = _whole(
        pack_own, [full(96), full(48), part(128)], core_arg, keys, values, _bf(_own_matrix()), scalars=1
    )
    r3, r6, late_cotangent = tie((r3, r6, cotangent))

    t1, t2 = _whole(pack_on, [full(136), full(72)], r3, r6, own1, own2, _bf(_pass_matrix()))
    t1, t2, late_cotangent = tie((t1, t2, late_cotangent))
    r2, r1 = hop(t2, 2), hop(t1, 1)
    split = late_cotangent.reshape(-1, 2 * n_head, half).transpose(1, 0, 2)
    do = lax.all_to_all(split, ("seq", "head"), 0, 0, axis_index_groups=chip_groups, tiled=True)
    do = do.reshape(2 * BLOCK, half)
    r1, r2, do = tie((r1, r2, do))
    mine, give = _whole(join_view, [view] * 2, core_arg, r1, r2, r3, r6, queries, scalars=1)
    other = swap(give)

    offsets, raise_by = _bias_tables()
    target = seq + (2 * core - 1) * jnp.asarray(offsets)
    bias = jnp.where((target >= 0) & (target < size), jnp.asarray(raise_by, f32), MASKED).astype(f32)

    step = PER_STEP * HEAD_DIM
    steps = half // step
    pick = pl.BlockSpec((2, BLOCK, step), lambda h, c: (0, 0, c[0] * steps + h))
    cut = lambda n: pl.BlockSpec((n, BLOCK, step), lambda h, c: (0, 0, h))
    const = lambda *dims: pl.BlockSpec(dims, lambda h, c: (0, 0))
    derive = _derive_matrix()
    spread = _own_matrix()[0:64, 0:BLOCK].T.copy()
    outs = [((2 * BLOCK, half), bf16), ((BLOCK, half), bf16)] + [part(BLOCK, f32)] * 2 + [((4, BLOCK, half), bf16), view]
    attended, dq_mine, gp, go, gx, gy = pl.pallas_call(
        attend,
        out_shape=[jax.ShapeDtypeStruct(s, d) for s, d in outs],
        grid_spec=pltpu.PrefetchScalarGridSpec(
            num_scalar_prefetch=1,
            grid=(steps,),
            in_specs=[pick] * 2
            + [pl.BlockSpec((2 * BLOCK, step), lambda h, c: (0, h)), cut(2), cut(5), cut(5)]
            + [const(192, 256), const(256, 192), const(128, 64), const(2, 640)],
            out_specs=[VMEM_SPEC] * len(outs),
        ),
        compiler_params=pltpu.CompilerParams(vmem_limit_bytes=WIDE_VMEM),
    )(core_arg, keys, values, do, ones, mine, other, _bf(derive), _bf(derive.T.copy()), _bf(spread), bias)

    take = swap(gy)
    u1, u2, far = _whole(split_view, [full(136), full(72), full(48)], core_arg, gx, take, scalars=1)
    u1, u2, attended = tie((u1, u2, attended))
    v2, v1 = hop(u2, -2), hop(u1, -1)
    out = lax.all_to_all(
        attended.reshape(2 * n_head, -1, half), ("seq", "head"), 0, 0, axis_index_groups=chip_groups, tiled=True
    )
    v1, v2, out = tie((v1, v2, out))

    u3, u6 = _whole(fold_on, [full(32), full(16)], far, v1, v2, _bf(_pass_matrix().T.copy()))
    v3, v6 = hop(u3, -3), hop(u6, -6)
    keep, back = _whole(
        fold_own, [full(BLOCK, f32), full(BLOCK)], core_arg, v1, v2, v3, v6, gp, go, _bf(_final_matrix()), scalars=1
    )
    back, out, dq_mine, dq_take = tie((back, out, dq_mine, take[4]))
    out = out.transpose(1, 0, 2).reshape(-1, n_head * width)
    query_gradient = jnp.concatenate(
        [jnp.where(core == 0, dq_mine, dq_take), jnp.where(core == 0, dq_take, dq_mine)], axis=1
    )
    key_gradient, value_gradient = pl.pallas_call(
        finish,
        out_shape=[jax.ShapeDtypeStruct((BLOCK, width), bf16)] * 2,
        in_specs=[VMEM_SPEC] * 2,
        compiler_params=pltpu.CompilerParams(vmem_limit_bytes=VMEM),
    )(keep, swap(back))
    return (out, query_gradient, key_gradient, value_gradient)


def solution(mesh):
    placed = (P("seq", "head"), P("seq", "head"), P("seq", "head"), P(("seq", "head"), None))
    return jax.shard_map(
        local,
        mesh=mesh,
        in_specs=placed,
        out_specs=(P(("seq", "head"), None), P("seq", "head"), P("seq", "head"), P("seq", "head")),
        check_vma=False,
    )
```
